128 devices in a mesh: inst: 4 (over x_hi, core), seq: 32 (over y, z, x_lo).
Axes of the slice: x: 4 (x_hi: 2, x_lo: 2; x = x_hi * 2 + x_lo), y: 4, z: 4, core: 2. Of those that a mesh axis runs over, the one named last changes fastest.
Arguments:
- query_rows: bfloat16 [16384, 8192], P(('inst', 'seq')), may hold values from -25 to 25
- key_rows: bfloat16 [16384, 1024], P(('inst', 'seq')), may hold values from -4 to 4
- value_rows: bfloat16 [16384, 1024], P(('inst', 'seq')), may hold values from -6 to 6
- target_instance: int32 [8192], P(('inst', 'seq')), may hold values from 0 to 3, as said below
- block_position: int32 [8192], P(('inst', 'seq')), may hold values from 0 to 2047, as said below
- request_lengths: int32 [4, 2], replicated, may hold values from 1 to 3584, 4096 in all within a row
Outputs:
- attended: bfloat16 [16384, 8192], P(('inst', 'seq'))
The draws below stay inside these ranges and needn't reach their ends.
Inputs may be any that keep to these rules, and one draw needn't show every extreme that they name: `target_instance`: together with block_position, every pair of an instance and a position block is named by exactly one entry block. Of the 64 blocks of one entry device, at most 1 name one instance and block positions b (values of block_position) with the same b // 64, and at most 1 name one instance and block positions with the same min(h, 63 - h), where h = b // 32; both bounds are reached. `block_position`: see target_instance.
All inputs are finite; a program needn't handle non-finite values.
Results may differ from the reference program's by a relative error of at most 0.0055.
Values may be sent and summed in bfloat16 or wider, within the bound.
No kernel may reach another device: no remote copies, remote signals or barrier semaphores. Data moves between devices by JAX's collectives and lax.ppermute only.
A program may use at most 128 MiB of HBM per device.

```python
import math
import jax
import jax.numpy as jnp
import numpy as np
from jax import lax

QUERY_HEADS = 64
KEY_HEADS = 8
HEAD_SIZE = 128
BLOCK_ROWS = 2
BLOCKS_DEV = 64
REQUESTS = 2
SEQUENCE = 4096
ALL_ROWS = 16384
LONGEST = 3584
N_INST = 4
N_SEQ = 32


def plan_tables(key):
    base = jax.random.fold_in(key, 11)
    streams = jax.random.split(base, 6)
    inst_count = N_INST
    seq_count = N_SEQ
    devices = inst_count * seq_count
    half_blocks = BLOCKS_DEV // 2
    capacity = BLOCKS_DEV // (2 * seq_count)
    class_size = inst_count // 2
    span = 2 * seq_count // inst_count
    shape = (devices, inst_count, span, capacity)
    source = lax.broadcasted_iota(jnp.int32, shape, 0)
    instance = lax.broadcasted_iota(jnp.int32, shape, 1)
    turn = lax.broadcasted_iota(jnp.int32, shape, 2)
    copies = lax.broadcasted_iota(jnp.int32, shape, 3)
    upper = source // seq_count
    lower = source % seq_count
    parity = (upper + instance) % 2
    pair_index = upper // 2 + class_size * turn
    offset = (lower + pair_index) % seq_count + seq_count * copies
    relabel_inst = jax.random.permutation(streams[0], inst_count).astype(jnp.int32)
    relabel_pair = jax.random.permutation(streams[1], seq_count).astype(jnp.int32)
    relabel_offset = jax.random.permutation(streams[2], half_blocks).astype(jnp.int32)
    flips = jax.random.randint(streams[3], (inst_count,), 0, 2).astype(jnp.int32)
    new_inst = relabel_inst[instance]
    halves = 2 * relabel_pair[pair_index] + (parity + flips[instance]) % 2
    position = halves * half_blocks + relabel_offset[offset]
    new_inst = new_inst.reshape(devices, BLOCKS_DEV)
    position = position.reshape(devices, BLOCKS_DEV)
    sources = jax.random.permutation(streams[4], devices).astype(jnp.int32)
    new_inst = new_inst[sources]
    position = position[sources]
    noise = jax.random.randint(streams[5], (devices, BLOCKS_DEV), 0, 1 << 20).astype(jnp.int32) * BLOCKS_DEV
    noise = noise + lax.broadcasted_iota(jnp.int32, (devices, BLOCKS_DEV), 1)
    ordering = jnp.argsort(noise, axis=1)
    new_inst = jnp.take_along_axis(new_inst, ordering, axis=1)
    position = jnp.take_along_axis(position, ordering, axis=1)
    return (new_inst.reshape(-1).astype(jnp.int32), position.reshape(-1).astype(jnp.int32))


def draw_target_instance(key, part):
    return plan_tables(key)[0]


def draw_block_position(key, part):
    return plan_tables(key)[1]


def draw_query_rows(key, part):
    streams = jax.random.split(jax.random.fold_in(key, 31), 1)
    width = QUERY_HEADS * HEAD_SIZE
    values = jnp.clip(1.5 * jax.random.normal(streams[0], (ALL_ROWS, width), jnp.float32), -6.0, 6.0)
    return values.astype(jnp.bfloat16)


def draw_key_rows(key, part):
    streams = jax.random.split(jax.random.fold_in(key, 37), 1)
    width = KEY_HEADS * HEAD_SIZE
    values = jnp.clip(jax.random.normal(streams[0], (ALL_ROWS, width), jnp.float32), -4.0, 4.0)
    return values.astype(jnp.bfloat16)


def block_scale(stream_key, extent, cuts, smallest, top_value):
    gain = 1.0
    for axis_at, blocks in cuts:
        heights = jax.random.uniform(jax.random.fold_in(jax.random.fold_in(stream_key, 6), axis_at), (blocks,), jnp.float32, smallest / len(cuts), top_value / len(cuts))
        gain = gain * jnp.repeat(jnp.exp(heights), extent[axis_at] // blocks).reshape((-1,) + (1,) * (len(extent) - 1 - axis_at))
    return gain


def profile(count, total, reach, lean):
    portions = [(1 << 20) // math.isqrt(grade ** lean) + 1 for grade in range(2, count + 1)]
    rest, counts = total - reach - (count - 1), [1] * (count - 1)
    while rest > 0:
        free = [i for i in range(count - 1) if counts[i] < reach]
        pool, remaining = sum([portions[i] for i in free]), rest
        for i in free:
            addition = min(reach - counts[i], max(1, remaining * portions[i] // pool), rest)
            counts[i] = counts[i] + addition
            rest = rest - addition
    return np.array([reach] + counts)


def uneven_parts(stream_key, amount, total, limit, slope):
    if amount == 2:
        one = jax.random.randint(stream_key, (), max(1, total - limit), min(limit, total - 1) + 1)
        return jnp.stack([one, total - one])
    lengths = jnp.asarray(profile(amount, total, limit, slope), jnp.int32)
    twos = (amount - 1) // 2
    giver, receiver = lengths[1:1 + 2 * twos:2], lengths[2:2 + 2 * twos:2]
    room = jnp.minimum(giver - 1, limit - receiver)
    moved = jax.random.randint(jax.random.fold_in(stream_key, 1), (twos,), 0, 1 << 20) % (room + 1)
    lengths = lengths.at[1:1 + 2 * twos:2].set(giver - moved).at[2:2 + 2 * twos:2].set(receiver + moved)
    return lengths[jax.random.permutation(jax.random.fold_in(stream_key, 2), amount)]


def gaussian(own_key, shape, deviation, limit, pieces=(), dtype=jnp.bfloat16):
    entries = jax.random.normal(own_key, shape, jnp.float32) * deviation
    if len(pieces) > 0:
        entries = block_scale(own_key, shape, pieces, -0.22, 0.18) * entries
    return jnp.clip(entries, min=-limit, max=limit).astype(dtype)


def setup_inputs(seed: int = 0) -> dict:
    key_of = jax.random.split(jax.random.key(seed), 7)
    query_rows = draw_query_rows(jax.random.fold_in(key_of[6], 71), 0)
    key_rows = draw_key_rows(jax.random.fold_in(key_of[6], 71), 0)
    value_rows = gaussian(key_of[2], (ALL_ROWS, KEY_HEADS * HEAD_SIZE), 1.0, 6.0, ((0, 128),))
    target_instance = draw_target_instance(jax.random.fold_in(key_of[6], 71), 0)
    block_position = draw_block_position(jax.random.fold_in(key_of[6], 71), 0)
    request_lengths = jax.vmap(lambda own: uneven_parts(own, REQUESTS, SEQUENCE, LONGEST, 2))(jax.random.split(key_of[5], N_INST)).reshape((N_INST, REQUESTS)).astype(jnp.int32)
    return {"query_rows": query_rows, "key_rows": key_rows, "value_rows": value_rows, "target_instance": target_instance, "block_position": block_position, "request_lengths": request_lengths}


def attend_instance(query_seq, key_seq, value_seq, lengths_here):
    groups = QUERY_HEADS // KEY_HEADS
    width = QUERY_HEADS * HEAD_SIZE
    score_scale = 1.0 / math.sqrt(HEAD_SIZE)
    request_ends = jnp.cumsum(lengths_here)
    positions = jnp.arange(SEQUENCE).astype(jnp.int32)
    starts = lax.optimization_barrier(jnp.sum(jnp.where(request_ends[None, :] <= positions[:, None], lengths_here[None, :], 0), axis=1)).astype(jnp.int32)
    key_heads = key_seq.reshape(SEQUENCE, KEY_HEADS, HEAD_SIZE).astype(jnp.float32)
    value_heads = value_seq.reshape(SEQUENCE, KEY_HEADS, HEAD_SIZE).astype(jnp.float32)
    block_size = 256 if SEQUENCE % 256 == 0 else 64

    def one_block(block_index):
        first = (block_index * block_size).astype(jnp.int32)
        query_block = lax.dynamic_slice_in_dim(query_seq, first, block_size, 0)
        query_heads = query_block.reshape(block_size, KEY_HEADS, groups, HEAD_SIZE).astype(jnp.float32)
        query_pos = first + jnp.arange(block_size).astype(jnp.int32)
        query_start = lax.dynamic_slice_in_dim(starts, first, block_size, 0)
        allowed = (positions[None, :] <= query_pos[:, None]) & (positions[None, :] >= query_start[:, None])
        scores = jnp.einsum('qhgd,khd->hgqk', query_heads, key_heads) * score_scale
        top = lax.optimization_barrier(jnp.max(jnp.where(allowed, scores, -1e+30), axis=-1))
        weights = jnp.where(allowed, jnp.exp(scores - top[..., None]), 0.0)
        totals = lax.optimization_barrier(jnp.sum(weights, axis=-1))
        rounded = lax.optimization_barrier(weights.astype(jnp.bfloat16)).astype(jnp.float32)
        mixed = jnp.einsum('hgqk,khd->hgqd', rounded, value_heads) / totals[..., None]
        return mixed.transpose(2, 0, 1, 3).reshape(block_size, width).astype(jnp.bfloat16)
    blocks_out = lax.map(one_block, jnp.arange(SEQUENCE // block_size).astype(jnp.int32))
    return blocks_out.reshape(SEQUENCE, width)

def reference(query_rows, key_rows, value_rows, target_instance, block_position, request_lengths):
    width = QUERY_HEADS * HEAD_SIZE
    row_ids = jnp.arange(ALL_ROWS).astype(jnp.int32)
    block_ids = row_ids // BLOCK_ROWS
    row_inst = target_instance[block_ids]
    row_pos = (block_position[block_ids] * BLOCK_ROWS + row_ids % BLOCK_ROWS).astype(jnp.int32)
    attended = jnp.zeros((ALL_ROWS, width), jnp.bfloat16)
    for which in range(N_INST):
        placed = jnp.where(row_inst == which, row_pos, SEQUENCE).astype(jnp.int32)
        query_seq = jnp.zeros((SEQUENCE, width), jnp.bfloat16).at[placed].set(query_rows, mode='drop')
        key_seq = jnp.zeros((SEQUENCE, KEY_HEADS * HEAD_SIZE), jnp.bfloat16).at[placed].set(key_rows, mode='drop')
        value_seq = jnp.zeros((SEQUENCE, KEY_HEADS * HEAD_SIZE), jnp.bfloat16).at[placed].set(value_rows, mode='drop')
        result = attend_instance(query_seq, key_seq, value_seq, request_lengths[which])
        attended = jnp.where((row_inst == which)[:, None], result[row_pos], attended)
    return attended
```

```python
import functools
import math

import jax
import jax.numpy as jnp
from jax import lax
from jax.experimental import pallas as pl
from jax.experimental.pallas import tpu as pltpu
from jax.sharding import PartitionSpec as P

BOTH = ("inst", "seq")
INSTANCES = 4
DEVICES = 128
KEY_HEADS = 8
HEAD = 128
BLOCKS = 64
ROWS = 128
CAP = 16
SLOTS = INSTANCES * CAP
SEQ_BLOCKS = 2048
POSITIONS = 4096
TILE = 256
TILES = SEQ_BLOCKS // TILE
SENT = 6 * CAP
CHUNK = SENT + 8
BACK = 4 * CAP
LOG2E = math.log2(math.e)
F32 = jnp.float32
BF16 = jnp.bfloat16


def ranks(plan):
    shape = (ROWS, ROWS)
    inst_l = jnp.broadcast_to(plan[0:1, :].astype(F32), shape)
    pos_l = jnp.broadcast_to(plan[1:2, :].astype(F32), shape)
    inst_s, pos_s = inst_l.T, pos_l.T
    lane = lax.broadcasted_iota(jnp.int32, shape, 1)
    sub = lax.broadcasted_iota(jnp.int32, shape, 0)
    same = inst_l == inst_s
    rank_l = jnp.sum(
        jnp.where(same & (pos_s < pos_l) & (sub % 2 == 0), 1.0, 0.0), axis=0, keepdims=True
    )
    rank_s = jnp.sum(
        jnp.where(same & (pos_l < pos_s) & (lane % 2 == 0), 1.0, 0.0), axis=1, keepdims=True
    )
    return inst_l, pos_l, inst_s, pos_s, rank_l, rank_s, lane, sub


def pack_kernel(first, plan_ref, q_ref, k_ref, v_ref, out_ref, pick_ref, label_ref):
    @pl.when(pl.program_id(0) == 0)
    def _():
        inst_l, _, inst_s, pos_s, rank_l, rank_s, lane, sub = ranks(plan_ref[...])
        turn = rank_l - first
        slot = jnp.where((turn >= 0) & (turn < CAP), inst_l[0:1] * CAP + turn, -1.0)
        hit = (jnp.broadcast_to(slot, (SLOTS, ROWS)) == sub[:SLOTS].astype(F32))
        for parity in range(2):
            pick_ref[parity] = jnp.where(hit & (lane[:SLOTS] % 2 == parity), 1.0, 0.0).astype(BF16)
        most = jnp.broadcast_to(jnp.max(rank_l, axis=1, keepdims=True) + 1.0, (8, ROWS))
        row = sub[:8]
        for i in range(INSTANCES):
            here = (inst_s == i) & (rank_s == lane.astype(F32)) & (sub % 2 == 0)
            block = jnp.sum(jnp.where(here, pos_s + 1.0, 0.0), axis=0, keepdims=True) - 1.0
            high = jnp.floor(block * (1.0 / 64.0))
            low = block - high * 64.0
            label = jnp.where(
                row == 0, jnp.broadcast_to(high, (8, ROWS)), jnp.broadcast_to(low, (8, ROWS))
            )
            label_ref[i] = jnp.where(row < 2, label, jnp.where(row == 2, most, 0.0)).astype(BF16)

    for parity in range(2):
        pick = pick_ref[parity]
        queries = jnp.dot(pick, q_ref[...], preferred_element_type=F32).astype(BF16)
        keys = jnp.dot(pick, k_ref[...], preferred_element_type=F32).astype(BF16)
        values = jnp.dot(pick, v_ref[...], preferred_element_type=F32).astype(BF16)
        for i in range(INSTANCES):
            rows = slice(i * CAP, (i + 1) * CAP)
            for r in range(4):
                to = (i // 2, r % 2, i % 2, 0, r // 2)
                for h in range(2):
                    at = (2 * parity + h) * CAP
                    head = (2 * r + h) * HEAD
                    out_ref[(*to, slice(at, at + CAP), slice(None))] = queries[rows, head : head + HEAD]
                if r % 2 == parity:
                    out_ref[(*to, slice(4 * CAP, 5 * CAP), slice(None))] = keys[rows]
                    out_ref[(*to, slice(5 * CAP, 6 * CAP), slice(None))] = values[rows]
                if parity == 0:
                    out_ref[(*to, slice(SENT, CHUNK), slice(None))] = label_ref[i]


def pack(turn, plan, q, k, v):
    group = 8 * HEAD
    return pl.pallas_call(
        functools.partial(pack_kernel, turn * CAP),
        grid=(KEY_HEADS,),
        in_specs=[
            pl.BlockSpec((2, ROWS), lambda g: (0, 0)),
            pl.BlockSpec((ROWS, group), lambda g: (0, g)),
            pl.BlockSpec((ROWS, HEAD), lambda g: (0, g)),
            pl.BlockSpec((ROWS, HEAD), lambda g: (0, g)),
        ],
        out_specs=pl.BlockSpec((2, 2, 2, 1, 2, CHUNK, HEAD), lambda g: (0, 0, 0, g, 0, 0, 0)),
        out_shape=jax.ShapeDtypeStruct((2, 2, 2, KEY_HEADS, 2, CHUNK, HEAD), BF16),
        scratch_shapes=[pltpu.VMEM((2, SLOTS, ROWS), BF16), pltpu.VMEM((INSTANCES, 8, ROWS), BF16)],
        name="pack",
    )(plan, q, k, v).reshape(DEVICES, CHUNK, HEAD)


def sort_kernel(parts, pos_ref, rows_ref, out_ref):
    slots = pos_ref.shape[1]
    wanted = lax.broadcasted_iota(jnp.int32, (TILE, slots), 0) + pl.program_id(0) * TILE
    pick = jnp.where(pos_ref[...] == wanted, 1.0, 0.0).astype(BF16)
    for c in range(0, parts, 2):
        pair = [rows_ref[:, p * CAP : (p + 1) * CAP, :].reshape(slots, HEAD) for p in (c, c + 1)]
        found = jnp.dot(pick, jnp.concatenate(pair, axis=1), preferred_element_type=F32).astype(BF16)
        out_ref[c] = found[:, :HEAD]
        out_ref[c + 1] = found[:, HEAD:]


def sort_rows(name, first, parts, pos_row, rows):
    slots = pos_row.shape[1]
    return pl.pallas_call(
        functools.partial(sort_kernel, parts),
        grid=(TILES,),
        in_specs=[
            pl.BlockSpec((1, slots), lambda t: (0, 0)),
            pl.BlockSpec((rows.shape[0], parts * CAP, HEAD), lambda t: (0, first // parts, 0)),
        ],
        out_specs=pl.BlockSpec((parts, TILE, HEAD), lambda t: (0, t, 0)),
        out_shape=jax.ShapeDtypeStruct((parts, SEQ_BLOCKS, HEAD), BF16),
        compiler_params=pltpu.CompilerParams(vmem_limit_bytes=40 << 20),
        cost_estimate=pl.CostEstimate(
            flops=2 * SEQ_BLOCKS * slots * parts * HEAD, bytes_accessed=4 << 20, transcendentals=0
        ),
        name=name,
    )(pos_row, rows)


def attend_kernel(facts_ref, q_ref, own_ref, other_ref, out_ref, top_ref, sum_ref):
    tile = pl.program_id(0)
    core = facts_ref[0]
    span = 2 * TILE
    queries = q_ref[...].reshape(4 * TILE, HEAD)
    scale = LOG2E / math.sqrt(HEAD)

    def start_of(position):
        start, end = jnp.int32(0), jnp.int32(0)
        for d in range(1, facts_ref.shape[0]):
            end = end + facts_ref[d]
            start = jnp.where(end <= position, end, start)
        return start

    def step(at, masked, fresh):
        keys_at = pl.ds(pl.multiple_of(at * TILE, TILE), TILE)
        keys = jnp.concatenate([own_ref[0, keys_at, :], other_ref[0, keys_at, :]], axis=0)
        values = jnp.concatenate([own_ref[1, keys_at, :], other_ref[1, keys_at, :]], axis=0)
        values = jnp.concatenate([values, jnp.ones((span, HEAD), BF16)], axis=1)
        scores = lax.dot_general(
            queries, keys, (((1,), (1,)), ((), ())), preferred_element_type=F32
        )
        if masked:
            row = lax.broadcasted_iota(jnp.int32, (4 * TILE, 1), 0)
            query_pos = tile * span + (row % TILE) * 2 + row // (2 * TILE)
            start, end = jnp.zeros_like(query_pos), jnp.int32(0)
            for d in range(1, facts_ref.shape[0]):
                end = end + facts_ref[d]
                start = jnp.where(end <= query_pos, end, start)
            lane = lax.broadcasted_iota(jnp.int32, (1, span), 1)
            parity = jnp.where(lane < TILE, core, 1 - core)
            key_pos = at * span + (lane % TILE) * 2 + parity
            scores = jnp.where((key_pos <= query_pos) & (key_pos >= start), scores, -1e30)
        best = jnp.max(scores, axis=1, keepdims=True) * scale
        if fresh:
            top = jnp.broadcast_to(best, (4 * TILE, HEAD))
        else:
            before = top_ref[...]
            top = jnp.maximum(before, best)
        weights = jnp.exp2(scores * scale - jnp.concatenate([top] * (span // HEAD), axis=1))
        added = jnp.dot(weights.astype(BF16), values, preferred_element_type=F32)
        if fresh:
            sum_ref[...] = added
        else:
            keep = jnp.exp2(before - top)
            sum_ref[...] = sum_ref[...] * jnp.concatenate([keep, keep], axis=1) + added
        top_ref[...] = top

    step(tile, True, True)
    low = start_of(tile * span) // span
    clear = jnp.clip((start_of(tile * span + span - 1) + span - 1) // span, low, tile)

    @pl.loop(low, clear)
    def _(at):
        step(at, True, False)

    @pl.loop(clear, tile)
    def _(at):
        step(at, False, False)

    done = sum_ref[:, :HEAD] / sum_ref[:, HEAD:]
    out_ref[...] = done.astype(BF16).reshape(4, TILE, HEAD)


def attend(facts, queries, own, other):
    return pl.pallas_call(
        attend_kernel,
        grid=(TILES,),
        in_specs=[
            pl.BlockSpec(memory_space=pltpu.SMEM),
            pl.BlockSpec((4, TILE, HEAD), lambda t: (0, t, 0)),
            pl.BlockSpec((2, SEQ_BLOCKS, HEAD), lambda t: (0, 0, 0)),
            pl.BlockSpec((2, SEQ_BLOCKS, HEAD), lambda t: (0, 0, 0)),
        ],
        out_specs=pl.BlockSpec((4, TILE, HEAD), lambda t: (0, t, 0)),
        out_shape=jax.ShapeDtypeStruct((4, SEQ_BLOCKS, HEAD), BF16),
        scratch_shapes=[
            pltpu.VMEM((4 * TILE, HEAD), F32),
            pltpu.VMEM((4 * TILE, 2 * HEAD), F32),
        ],
        compiler_params=pltpu.CompilerParams(vmem_limit_bytes=48 << 20),
        name="attend",
    )(facts, queries, own, other)


def unsort_kernel(pos_ref, rows_ref, out_ref):
    block = lax.broadcasted_iota(jnp.int32, (TILE, SEQ_BLOCKS), 1)
    pick = jnp.where(pos_ref[...] == block, 1.0, 0.0).astype(BF16)
    for c in range(0, 4, 2):
        pair = jnp.concatenate([rows_ref[c], rows_ref[c + 1]], axis=1)
        found = jnp.dot(pick, pair, preferred_element_type=F32).astype(BF16)
        for p in range(2):
            part = found[:, p * HEAD : (p + 1) * HEAD].reshape(TILE // CAP, CAP, HEAD)
            out_ref[:, (c + p) * CAP : (c + p + 1) * CAP, :] = part


def unsort_rows(pos_column, rows):
    slots = pos_column.shape[0]
    return pl.pallas_call(
        unsort_kernel,
        grid=(slots // TILE,),
        in_specs=[
            pl.BlockSpec((TILE, 1), lambda t: (t, 0)),
            pl.BlockSpec((4, SEQ_BLOCKS, HEAD), lambda t: (0, 0, 0)),
        ],
        out_specs=pl.BlockSpec((TILE // CAP, BACK, HEAD), lambda t: (t, 0, 0)),
        out_shape=jax.ShapeDtypeStruct((slots // CAP, BACK, HEAD), BF16),
        compiler_params=pltpu.CompilerParams(vmem_limit_bytes=40 << 20),
        name="unsort",
    )(pos_column, rows)


def unpack_kernel(rounds, plan_ref, *refs):
    back_refs, out_ref, place_ref = refs[:rounds], refs[rounds], refs[rounds + 1]

    @pl.when(pl.program_id(0) == 0)
    def _():
        _, _, inst_s, _, _, rank_s, lane, sub = ranks(plan_ref[...])
        for turn in range(rounds):
            step = rank_s - turn * CAP
            slot = jnp.where((step >= 0) & (step < CAP), inst_s[:, :SLOTS] * CAP + step, -1.0)
            hit = slot == lane[:, :SLOTS].astype(F32)
            for parity in range(2):
                place_ref[turn, parity] = jnp.where(
                    hit & (sub[:, :SLOTS] % 2 == parity), 1.0, 0.0
                ).astype(BF16)

    total = jnp.zeros(out_ref.shape, F32)
    for turn in range(rounds):
        for parity in range(2):
            lines = []
            for i in range(INSTANCES):
                line = []
                for r in range(4):
                    of = (i // 2, r % 2, i % 2, 0, r // 2)
                    for h in range(2):
                        at = (2 * parity + h) * CAP
                        line.append(back_refs[turn][(*of, slice(at, at + CAP), slice(None))])
                lines.append(jnp.concatenate(line, axis=1))
            total = total + jnp.dot(
                place_ref[turn, parity], jnp.concatenate(lines, axis=0), preferred_element_type=F32
            )
    out_ref[...] = total.astype(BF16)


def unpack(plan, backs):
    group = 8 * HEAD
    rounds = len(backs)
    return pl.pallas_call(
        functools.partial(unpack_kernel, rounds),
        grid=(KEY_HEADS,),
        in_specs=[pl.BlockSpec((2, ROWS), lambda g: (0, 0))]
        + [pl.BlockSpec((2, 2, 2, 1, 2, BACK, HEAD), lambda g: (0, 0, 0, g, 0, 0, 0))] * rounds,
        out_specs=pl.BlockSpec((ROWS, group), lambda g: (0, g)),
        out_shape=jax.ShapeDtypeStruct((ROWS, KEY_HEADS * group), BF16),
        scratch_shapes=[pltpu.VMEM((rounds, 2, ROWS, SLOTS), BF16)],
        name="unpack",
    )(plan, *(b.reshape(2, 2, 2, KEY_HEADS, 2, BACK, HEAD) for b in backs))


def exchange(x):
    return lax.all_to_all(x, BOTH, split_axis=0, concat_axis=0, tiled=True)


def shards(query_rows, key_rows, value_rows, target_instance, block_position, request_lengths):
    spot = lax.axis_index("inst")
    core = spot % 2
    instance = (spot // 2) * 2 + lax.axis_index("seq") // 16
    plan = jnp.repeat(jnp.stack([target_instance, block_position]), 2, axis=1)
    lengths = lax.dynamic_index_in_dim(request_lengths, instance, 0, keepdims=False)
    facts = jnp.concatenate([core[None], lengths]).astype(jnp.int32)

    got = exchange(pack(0, plan, query_rows, key_rows, value_rows))
    labels = got[:, SENT : SENT + 3, : 2 * CAP].astype(jnp.int32)
    positions = labels[:, 0] * 64 + labels[:, 1]
    most = jnp.max(labels[:, 2, 0])

    def finish(rounds):
        rows, where = got, positions[:, :CAP].reshape(-1)
        if rounds == 2:
            more = exchange(pack(1, plan, query_rows, key_rows, value_rows))
            rows = jnp.concatenate([rows, more], axis=0)
            where = jnp.concatenate([where, positions[:, CAP:].reshape(-1)])
        pos_row, pos_column = where[None, :], where[:, None]
        own = sort_rows("sort_keys", 4, 2, pos_row, rows)
        other = lax.ppermute(own, "inst", [(0, 1), (1, 0), (2, 3), (3, 2)])
        queries = sort_rows("sort_queries", 0, 4, pos_row, rows)
        sorted_out = attend(facts, queries, own, other)
        back = unsort_rows(pos_column, sorted_out)
        backs = [exchange(back[t * DEVICES : (t + 1) * DEVICES]) for t in range(rounds)]
        return unpack(plan, backs)

    return lax.cond(most > CAP, lambda: finish(2), lambda: finish(1))


def solution(mesh):
    rows = P(BOTH, None)
    return jax.shard_map(
        shards,
        mesh=mesh,
        in_specs=(rows, rows, rows, P(BOTH), P(BOTH), P()),
        out_specs=rows,
        check_vma=False,
    )
```

```python
import functools
import math

import jax
import jax.numpy as jnp
from jax import lax
from jax.experimental import pallas as pl
from jax.experimental.pallas import tpu as pltpu
from jax.sharding import PartitionSpec as P

BOTH = ("inst", "seq")
INSTANCES = 4
DEVICES = 128
KEY_HEADS = 8
HEAD = 128
ROWS = 128
CAP = 16
SLOTS = INSTANCES * CAP
SEQ_BLOCKS = 2048
TILE = 256
TILES = SEQ_BLOCKS // TILE
SORTED = 512
SENT = 6 * CAP
CHUNK = SENT + 8
BACK = 4 * CAP
GROUP = 2
WIDE = GROUP * 8 * HEAD
SCALE = math.log2(math.e) / math.sqrt(HEAD)
ROOM = pltpu.CompilerParams(vmem_limit_bytes=58 << 20)
F32 = jnp.float32
BF16 = jnp.bfloat16


def ranks(facts_ref):
    shape = (ROWS, ROWS)
    inst_l = jnp.broadcast_to(facts_ref[0:1, :].astype(F32), shape)
    pos_l = jnp.broadcast_to(facts_ref[1:2, :].astype(F32), shape)
    inst_s, pos_s = inst_l.T, pos_l.T
    lane = lax.broadcasted_iota(jnp.int32, shape, 1)
    sub = lax.broadcasted_iota(jnp.int32, shape, 0)
    same = inst_l == inst_s
    rank_l = jnp.sum(
        jnp.where(same & (pos_s < pos_l) & (sub % 2 == 0), 1.0, 0.0), axis=0, keepdims=True
    )
    rank_s = jnp.sum(
        jnp.where(same & (pos_l < pos_s) & (lane % 2 == 0), 1.0, 0.0), axis=1, keepdims=True
    )
    return inst_l, inst_s, pos_s, rank_l, rank_s, lane, sub


def pack_kernel(turn, plan_ref, q_ref, k_ref, v_ref, out_ref, pick_ref, label_ref):
    @pl.when(pl.program_id(0) == 0)
    def _():
        inst_l, inst_s, pos_s, rank_l, rank_s, lane, sub = ranks(plan_ref)
        step = rank_l - turn * CAP
        slot = jnp.where((step >= 0) & (step < CAP), inst_l[0:1] * CAP + step, -1.0)
        hit = (slot == (sub % SLOTS).astype(F32)) & (lane % 2 == sub // SLOTS)
        pick_ref[...] = jnp.where(hit, 1.0, 0.0).astype(BF16)
        most = jnp.max(rank_l, axis=1, keepdims=True) + 1.0
        row = sub[:8]
        place = lane - plan_ref[2:3, :]
        for i in range(INSTANCES):
            label = jnp.where(row == 4, most, 0.0)
            for t in range(2):
                here = (inst_s == i) & (rank_s == (place + t * CAP).astype(F32))
                here = here & (place >= 0) & (place < CAP) & (sub % 2 == 0)
                block = jnp.sum(jnp.where(here, pos_s + 1.0, 0.0), axis=0, keepdims=True)
                high = jnp.floor(block * (1.0 / 64.0))
                label = jnp.where(row == 2 * t, high, label)
                label = jnp.where(row == 2 * t + 1, block - high * 64.0, label)
            label_ref[i] = label.astype(BF16)

    pick = pick_ref[...]
    queries = jnp.dot(pick, q_ref[...], preferred_element_type=F32).astype(BF16)
    keys = jnp.dot(pick, k_ref[...], preferred_element_type=F32).astype(BF16)
    values = jnp.dot(pick, v_ref[...], preferred_element_type=F32).astype(BF16)
    for i in range(INSTANCES):
        for g in range(GROUP):
            for r in range(4):
                to = (i // 2, r % 2, i % 2, g, r // 2)
                for c in range(4):
                    at = (c // 2) * SLOTS + i * CAP
                    head = (8 * g + 2 * r + c % 2) * HEAD
                    out_ref[(*to, slice(c * CAP, (c + 1) * CAP), slice(None))] = queries[
                        at : at + CAP, head : head + HEAD
                    ]
                at = (r % 2) * SLOTS + i * CAP
                lanes = slice(g * HEAD, (g + 1) * HEAD)
                out_ref[(*to, slice(4 * CAP, 5 * CAP), slice(None))] = keys[at : at + CAP, lanes]
                out_ref[(*to, slice(5 * CAP, 6 * CAP), slice(None))] = values[at : at + CAP, lanes]
                out_ref[(*to, slice(SENT, CHUNK), slice(None))] = label_ref[i]


def pack(turn, plan, q, k, v):
    return pl.pallas_call(
        functools.partial(pack_kernel, turn),
        grid=(KEY_HEADS // GROUP,),
        in_specs=[
            pl.BlockSpec((3, ROWS), lambda g: (0, 0)),
            pl.BlockSpec((ROWS, WIDE), lambda g: (0, g)),
            pl.BlockSpec((ROWS, GROUP * HEAD), lambda g: (0, g)),
            pl.BlockSpec((ROWS, GROUP * HEAD), lambda g: (0, g)),
        ],
        out_specs=pl.BlockSpec((2, 2, 2, GROUP, 2, CHUNK, HEAD), lambda g: (0, 0, 0, g, 0, 0, 0)),
        out_shape=jax.ShapeDtypeStruct((2, 2, 2, KEY_HEADS, 2, CHUNK, HEAD), BF16),
        scratch_shapes=[pltpu.VMEM((ROWS, ROWS), BF16), pltpu.VMEM((INSTANCES, 8, ROWS), BF16)],
        compiler_params=ROOM,
        name="pack",
    )(plan, q, k, v).reshape(DEVICES, CHUNK, HEAD)


def slot_positions(turn, rows_ref):
    label = rows_ref[:, SENT:CHUNK, :].astype(F32).reshape(DEVICES // 8, 8, 8, HEAD)
    label = jnp.sum(label, axis=1)
    row = lax.broadcasted_iota(jnp.int32, label.shape, 1)
    part = jnp.where(row == 2 * turn, label * 64.0, jnp.where(row == 2 * turn + 1, label, 0.0))
    return jnp.sum(part, axis=1) - 1.0


def line_up(pos):
    return jnp.concatenate([pos[j : j + 1] for j in range(DEVICES // 8)], axis=1)


def sorted_pair(line_ref, rows_refs, c):
    slots = DEVICES * CAP
    wanted = lax.broadcasted_iota(jnp.int32, (SORTED, slots), 0) + pl.program_id(0) * SORTED
    found = None
    for turn, rows_ref in enumerate(rows_refs):
        pick = jnp.where(line_ref[turn, 0:1, :] == wanted, 1.0, 0.0).astype(BF16)
        pair = [rows_ref[:, p * CAP : (p + 1) * CAP, :].reshape(slots, HEAD) for p in (c, c + 1)]
        added = jnp.dot(pick, jnp.concatenate(pair, axis=1), preferred_element_type=F32)
        found = added if found is None else found + added
    return found


def sort_keys_kernel(rounds, *refs):
    rows_refs = refs[:rounds]
    keys_ref, values_ref, line_ref, column_ref, most_ref = refs[rounds:]

    @pl.when(pl.program_id(0) == 0)
    def _():
        for turn in range(rounds):
            pos = slot_positions(turn, rows_refs[0])
            line_ref[turn] = jnp.broadcast_to(line_up(pos).astype(jnp.int32), (8, DEVICES * CAP))
            empty = jnp.zeros((HEAD - DEVICES // 8, HEAD), F32)
            column_ref[turn] = jnp.concatenate([pos, empty], axis=0).T
        count = rows_refs[0][:, SENT:CHUNK, :].astype(F32)
        row = lax.broadcasted_iota(jnp.int32, count.shape, 1)
        most_ref[0] = jnp.max(jnp.where(row == 4, count, 0.0)).astype(jnp.int32)

    found = sorted_pair(line_ref, rows_refs, 4)
    keys_ref[...] = found[:, :HEAD].astype(BF16)
    values_ref[...] = found[:, HEAD:].T.astype(BF16)


def sort_keys(rows):
    rounds, slots = len(rows), DEVICES * CAP
    line, column = (rounds, 8, slots), (rounds, HEAD, HEAD)
    return pl.pallas_call(
        functools.partial(sort_keys_kernel, rounds),
        grid=(SEQ_BLOCKS // SORTED,),
        in_specs=[pl.BlockSpec((DEVICES, CHUNK, HEAD), lambda t: (0, 0, 0))] * rounds,
        out_specs=(
            pl.BlockSpec((SORTED, HEAD), lambda t: (t, 0)),
            pl.BlockSpec((HEAD, SORTED), lambda t: (0, t)),
            pl.BlockSpec(line, lambda t: (0, 0, 0)),
            pl.BlockSpec(column, lambda t: (0, 0, 0)),
            pl.BlockSpec(memory_space=pltpu.SMEM),
        ),
        out_shape=(
            jax.ShapeDtypeStruct((SEQ_BLOCKS, HEAD), BF16),
            jax.ShapeDtypeStruct((HEAD, SEQ_BLOCKS), BF16),
            jax.ShapeDtypeStruct(line, jnp.int32),
            jax.ShapeDtypeStruct(column, F32),
            jax.ShapeDtypeStruct((1,), jnp.int32),
        ),
        compiler_params=ROOM,
        name="sort_keys",
    )(*rows)


def sort_queries_kernel(line_ref, *refs):
    out_ref = refs[-1]
    for c in range(0, 4, 2):
        found = sorted_pair(line_ref, refs[:-1], c).astype(BF16)
        out_ref[c] = found[:, :HEAD]
        out_ref[c + 1] = found[:, HEAD:]


def sort_queries(line, rows):
    flops = 2 * SEQ_BLOCKS * DEVICES * CAP * len(rows) * 4 * HEAD
    return pl.pallas_call(
        sort_queries_kernel,
        grid=(SEQ_BLOCKS // SORTED,),
        in_specs=[pl.BlockSpec(line.shape, lambda t: (0, 0, 0))]
        + [pl.BlockSpec((DEVICES, 4 * CAP, HEAD), lambda t: (0, 0, 0))] * len(rows),
        out_specs=pl.BlockSpec((4, SORTED, HEAD), lambda t: (0, t, 0)),
        out_shape=jax.ShapeDtypeStruct((4, SEQ_BLOCKS, HEAD), BF16),
        compiler_params=ROOM,
        cost_estimate=pl.CostEstimate(flops=flops, bytes_accessed=4 << 20, transcendentals=0),
        name="sort_queries",
    )(line, *rows)


def attend_tile(
    tile, facts_ref, q_ref, own_keys, own_values, other_keys, other_values, out_ref, sum_ref, top_ref
):
    core = facts_ref[0]
    span = 2 * TILE
    columns = 4 * TILE
    first = tile * span

    def start_of(position):
        start, end = jnp.zeros_like(position), jnp.int32(0)
        for d in range(1, facts_ref.shape[0]):
            end = end + facts_ref[d]
            start = jnp.where(end <= position, end, start)
        return start

    column = lax.broadcasted_iota(jnp.int32, (1, columns), 1)
    query_pos = first + (column % TILE) * 2 + column // (2 * TILE)
    query_start = start_of(query_pos)

    def key_pos(at, index):
        own = index < TILE
        block = jnp.where(own, index, index - TILE) + at * TILE
        return block * 2 + jnp.where(own, core, 1 - core)

    def scores_of(at, wide):
        at_keys = pl.ds(pl.multiple_of(at * TILE, TILE), wide * TILE)
        keys = jnp.concatenate([own_keys[at_keys, :], other_keys[at_keys, :]], axis=0)
        scores = lax.dot_general(
            keys,
            q_ref[...].reshape(columns, HEAD),
            (((1,), (1,)), ((), ())),
            preferred_element_type=F32,
        )
        return scores * SCALE

    def allowed(at, whole):
        pos = key_pos(at, lax.broadcasted_iota(jnp.int32, (span, 1), 0))
        return (pos <= query_pos) & (pos >= query_start) if whole else pos <= query_pos

    def mixed(at, wide, weights, start=None):
        at_keys = pl.ds(pl.multiple_of(at * TILE, TILE), wide * TILE)
        values = jnp.concatenate([own_values[:, at_keys], other_values[:, at_keys]], axis=1)
        ones = jnp.ones((16, wide * span), BF16)
        if start is not None:
            pos = key_pos(at, lax.broadcasted_iota(jnp.int32, (16, span), 1))
            ones = jnp.where(pos >= start, 1.0, 0.0).astype(BF16)
            values = values * ones[0:1]
        values = jnp.concatenate([values, ones], axis=0)
        return jnp.dot(values, weights.astype(BF16), preferred_element_type=F32)

    start = start_of(first)
    low = start // span
    clear = jnp.minimum((start + span - 1) // span, tile)
    split = start_of(first + span - 1) > first

    def plain(at, wide, start=None):
        sum_ref[...] += mixed(at, wide, jnp.exp2(scores_of(at, wide)), start)

    sum_ref[...] = jnp.zeros_like(sum_ref)

    @pl.when(low < clear)
    def _():
        plain(low, 1, start)

    left = tile - clear
    for wide in (1, 2, 4):

        @pl.when((left // wide) % 2 == 1)
        def _():
            plain(clear + left % wide, wide)

    def diagonal(whole):
        weights = jnp.exp2(jnp.where(allowed(tile, whole), scores_of(tile, 1), -1e30))
        added = mixed(tile, 1, weights)
        if whole:
            sum_ref[...] = jnp.where(query_start <= first, sum_ref[...], 0.0) + added
        else:
            sum_ref[...] += added

    @pl.when(split)
    def _():
        diagonal(True)

    @pl.when(jnp.logical_not(split))
    def _():
        diagonal(False)

    total = sum_ref[HEAD : HEAD + 8]
    fine = (jnp.max(total) <= 2.0**100) & (jnp.min(total) >= 2.0**-80)

    @pl.when(jnp.logical_not(fine))
    def _():
        def shifted(at, begins):
            scores = jnp.where(allowed(at, True), scores_of(at, 1), -1e30)
            best = jnp.broadcast_to(jnp.max(scores, axis=0, keepdims=True), (8, columns))
            top = best if begins else jnp.maximum(top_ref[...], best)
            added = mixed(at, 1, jnp.exp2(scores - top[0:1]))
            if begins:
                sum_ref[...] = added
            else:
                sum_ref[...] = sum_ref[...] * jnp.exp2(top_ref[0:1] - top[0:1]) + added
            top_ref[...] = top

        shifted(tile, True)

        @pl.loop(low, tile)
        def _(at):
            shifted(at, False)

    done = (sum_ref[:HEAD] / sum_ref[HEAD : HEAD + 1]).astype(BF16)
    place = pl.ds(pl.multiple_of(tile * TILE, TILE), TILE)
    for c in range(4):
        out_ref[c * HEAD : (c + 1) * HEAD, place] = done[:, c * TILE : (c + 1) * TILE]


def unsort_tile(tile, column_ref, attended_ref, out_ref):
    lane = lax.broadcasted_iota(jnp.int32, (HEAD, HEAD), 1)
    turn, near = tile // TILES, tile % TILES
    columns = [
        jnp.sum(jnp.where(lane == near * 2 + j, column_ref[turn], 0.0), axis=1, keepdims=True)
        for j in range(2)
    ]
    pos = jnp.concatenate(columns, axis=0).astype(jnp.int32)
    block = lax.broadcasted_iota(jnp.int32, (TILE, SEQ_BLOCKS), 1)
    pick = jnp.where(pos == block, 1.0, 0.0).astype(BF16)
    for c in range(0, 4, 2):
        found = lax.dot_general(
            pick,
            attended_ref[c * HEAD : (c + 2) * HEAD, :],
            (((1,), (1,)), ((), ())),
            preferred_element_type=F32,
        ).astype(BF16)
        for p in range(2):
            part = found[:, p * HEAD : (p + 1) * HEAD].reshape(TILE // CAP, CAP, HEAD)
            out_ref[:, (c + p) * CAP : (c + p + 1) * CAP, :] = part


def attend_kernel(facts_ref, column_ref, q_ref, *refs):
    key_refs, out_ref, attended_ref, more = refs[:4], refs[4], refs[5], refs[6:]
    step = pl.program_id(0)

    @pl.when(step < TILES)
    def _():
        attend_tile(step, facts_ref, q_ref, *key_refs, attended_ref, *more)

    @pl.when(step >= TILES)
    def _():
        unsort_tile(step - TILES, column_ref, attended_ref, out_ref)


def attend(facts, column, queries, own, other):
    rounds = column.shape[0]
    keys = pl.BlockSpec((SEQ_BLOCKS, HEAD), lambda t: (0, 0))
    values = pl.BlockSpec((HEAD, SEQ_BLOCKS), lambda t: (0, 0))
    return pl.pallas_call(
        attend_kernel,
        grid=(TILES + rounds * TILES,),
        in_specs=[
            pl.BlockSpec(memory_space=pltpu.SMEM),
            pl.BlockSpec(column.shape, lambda t: (0, 0, 0)),
            pl.BlockSpec((4, TILE, HEAD), lambda t: (0, jnp.minimum(t, TILES - 1), 0)),
            keys,
            values,
            keys,
            values,
        ],
        out_specs=pl.BlockSpec(
            (DEVICES // TILES, BACK, HEAD), lambda t: (jnp.maximum(t - TILES, 0), 0, 0)
        ),
        out_shape=jax.ShapeDtypeStruct((rounds * DEVICES, BACK, HEAD), BF16),
        scratch_shapes=[
            pltpu.VMEM((4 * HEAD, SEQ_BLOCKS), BF16),
            pltpu.VMEM((HEAD + 16, 4 * TILE), F32),
            pltpu.VMEM((8, 4 * TILE), F32),
        ],
        compiler_params=ROOM,
        name="attend",
    )(facts, column, queries, *own, *other)


def unpack_kernel(rounds, plan_ref, *refs):
    back_refs, out_ref, place_ref = refs[:rounds], refs[rounds], refs[rounds + 1]

    @pl.when(pl.program_id(0) == 0)
    def _():
        _, inst_s, _, _, rank_s, lane, sub = ranks(plan_ref)
        for turn in range(rounds):
            step = rank_s - turn * CAP
            slot = jnp.where((step >= 0) & (step < CAP), inst_s * CAP + step, -1.0)
            hit = (slot == (lane % SLOTS).astype(F32)) & (sub % 2 == lane // SLOTS)
            place_ref[turn] = jnp.where(hit, 1.0, 0.0).astype(BF16)

    total = jnp.zeros(out_ref.shape, F32)
    for turn in range(rounds):
        lines = []
        for parity in range(2):
            for i in range(INSTANCES):
                line = []
                for g in range(GROUP):
                    for r in range(4):
                        of = (i // 2, r % 2, i % 2, g, r // 2)
                        for h in range(2):
                            at = (2 * parity + h) * CAP
                            line.append(back_refs[turn][(*of, slice(at, at + CAP), slice(None))])
                lines.append(jnp.concatenate(line, axis=1))
        total = total + jnp.dot(
            place_ref[turn], jnp.concatenate(lines, axis=0), preferred_element_type=F32
        )
    out_ref[...] = total.astype(BF16)


def unpack(plan, backs):
    rounds = len(backs)
    block = pl.BlockSpec((2, 2, 2, GROUP, 2, BACK, HEAD), lambda g: (0, 0, 0, g, 0, 0, 0))
    return pl.pallas_call(
        functools.partial(unpack_kernel, rounds),
        grid=(KEY_HEADS // GROUP,),
        in_specs=[pl.BlockSpec((3, ROWS), lambda g: (0, 0))] + [block] * rounds,
        out_specs=pl.BlockSpec((ROWS, WIDE), lambda g: (0, g)),
        out_shape=jax.ShapeDtypeStruct((ROWS, KEY_HEADS * 8 * HEAD), BF16),
        scratch_shapes=[pltpu.VMEM((rounds, ROWS, ROWS), BF16)],
        compiler_params=ROOM,
        name="unpack",
    )(plan, *(b.reshape(2, 2, 2, KEY_HEADS, 2, BACK, HEAD) for b in backs))


def exchange(x):
    return lax.all_to_all(x, BOTH, split_axis=0, concat_axis=0, tiled=True)


def shards(query_rows, key_rows, value_rows, target_instance, block_position, request_lengths):
    spot, place = lax.axis_index("inst"), lax.axis_index("seq")
    core = spot % 2
    instance = (spot // 2) * 2 + place // 16
    offset = jnp.full_like(block_position, (place % 8) * CAP)
    plan = jnp.repeat(jnp.stack([target_instance, block_position, offset]), 2, axis=1)
    lengths = lax.dynamic_index_in_dim(request_lengths, instance, 0, keepdims=False)
    facts = jnp.concatenate([core[None], lengths]).astype(jnp.int32)

    def run(rounds):
        rows = [exchange(pack(t, plan, query_rows, key_rows, value_rows)) for t in range(rounds)]
        keys, values, line, column, most = sort_keys(rows)
        pairs = [(0, 1), (1, 0), (2, 3), (3, 2)]
        other = [lax.ppermute(x, "inst", pairs) for x in (keys, values)]
        back = attend(facts, column, sort_queries(line, rows), (keys, values), other)
        backs = [exchange(back[t * DEVICES : (t + 1) * DEVICES]) for t in range(rounds)]
        return unpack(plan, backs), most[0]

    attended, most = run(1)
    return lax.while_loop(
        lambda state: state[1] > CAP,
        lambda state: (run(2)[0], jnp.zeros_like(state[1])),
        (attended, most),
    )[0]


def solution(mesh):
    rows = P(BOTH, None)
    return jax.shard_map(
        shards,
        mesh=mesh,
        in_specs=(rows, rows, rows, P(BOTH), P(BOTH), P()),
        out_specs=rows,
        check_vma=False,
    )
```

```python
import functools
import math

import jax
import jax.numpy as jnp
from jax import lax
from jax.experimental import pallas as pl
from jax.experimental.pallas import tpu as pltpu
from jax.sharding import PartitionSpec as P

BOTH = ("inst", "seq")
INSTANCES = 4
DEVICES = 128
KEY_HEADS = 8
HEAD = 128
ROWS = 128
CAP = 16
SLOTS = INSTANCES * CAP
SEQ_BLOCKS = 2048
TILE = 256
TILES = SEQ_BLOCKS // TILE
SORTED = 1024
TURNS = 2
UNSORTED = 1024
UNSORTS = DEVICES * CAP // UNSORTED
SENT = 6 * CAP
CHUNK = SENT + 8
BACK = 4 * CAP
GROUP = 4
WIDE = GROUP * 8 * HEAD
SCALE = math.log2(math.e) / math.sqrt(HEAD)
ROOM = pltpu.CompilerParams(vmem_limit_bytes=36 << 20)
F32 = jnp.float32
BF16 = jnp.bfloat16


def plan_pack(turn, facts_ref, target_ref, block_ref, pick_ref, label_ref, place_ref):
    shape = (ROWS, ROWS)
    half = jnp.full((1, ROWS // 2), -1.0, F32)
    inst_l = jnp.concatenate([target_ref[...].astype(F32), half], axis=1)
    pos_l = jnp.concatenate([block_ref[...].astype(F32), half], axis=1)
    inst_s, pos_s = jnp.broadcast_to(inst_l, shape).T, jnp.broadcast_to(pos_l, shape).T
    lane = lax.broadcasted_iota(jnp.int32, shape, 1)
    sub = lax.broadcasted_iota(jnp.int32, shape, 0)
    ahead = (inst_l == inst_s) & (pos_l < pos_s)
    rank = jnp.sum(jnp.where(ahead, 1.0, 0.0), axis=1, keepdims=True)
    step = rank - turn * CAP
    slot = jnp.where((step >= 0) & (step < CAP), inst_s * CAP + step, -1.0)
    slot = jnp.sum(jnp.where(lane // 2 == sub, slot, 0.0), axis=0, keepdims=True)
    hit = (slot == (sub % SLOTS).astype(F32)) & (lane % 2 == sub // SLOTS)
    pick = jnp.where(hit, 1.0, 0.0)
    pick_ref[...] = pick.astype(BF16)
    place_ref[...] = pick.T.astype(BF16)
    most = jnp.max(jnp.broadcast_to(rank, shape), axis=0, keepdims=True) + 1.0
    row = sub[:8]
    at = lane - facts_ref[1]
    for i in range(INSTANCES):
        label = jnp.where(row == 4, most, 0.0)
        for t in range(2):
            here = (inst_s == i) & (rank == (at + t * CAP).astype(F32)) & (at >= 0) & (at < CAP)
            block = jnp.sum(jnp.where(here, pos_s + 1.0, 0.0), axis=0, keepdims=True)
            high = jnp.floor(block * (1.0 / 64.0))
            label = jnp.where(row == 2 * t, high, label)
            label = jnp.where(row == 2 * t + 1, block - high * 64.0, label)
        label_ref[i] = label.astype(BF16)


def pack_kernel(turn, facts_ref, target_ref, block_ref, q_ref, k_ref, v_ref, out_ref, place_ref, pick_ref, label_ref):
    @pl.when(pl.program_id(0) == 0)
    def _():
        plan_pack(turn, facts_ref, target_ref, block_ref, pick_ref, label_ref, place_ref)

    pick = pick_ref[...]
    queries = jnp.dot(pick, q_ref[...], preferred_element_type=F32).astype(BF16)
    keys = jnp.dot(pick, k_ref[...], preferred_element_type=F32).astype(BF16)
    values = jnp.dot(pick, v_ref[...], preferred_element_type=F32).astype(BF16)
    for i in range(INSTANCES):
        for g in range(GROUP):
            for r in range(4):
                to = (i // 2, r % 2, i % 2, g, r // 2)
                for c in range(4):
                    at = (c // 2) * SLOTS + i * CAP
                    head = (8 * g + 2 * r + c % 2) * HEAD
                    out_ref[(*to, slice(c * CAP, (c + 1) * CAP), slice(None))] = queries[
                        at : at + CAP, head : head + HEAD
                    ]
                at = (r % 2) * SLOTS + i * CAP
                lanes = slice(g * HEAD, (g + 1) * HEAD)
                out_ref[(*to, slice(4 * CAP, 5 * CAP), slice(None))] = keys[at : at + CAP, lanes]
                out_ref[(*to, slice(5 * CAP, 6 * CAP), slice(None))] = values[at : at + CAP, lanes]
                out_ref[(*to, slice(SENT, CHUNK), slice(None))] = label_ref[i]


def pack(turn, facts, target, block, q, k, v):
    rows, place = pl.pallas_call(
        functools.partial(pack_kernel, turn),
        grid=(KEY_HEADS // GROUP,),
        in_specs=[
            pl.BlockSpec(memory_space=pltpu.SMEM),
            pl.BlockSpec((1, ROWS // 2), lambda g: (0, 0)),
            pl.BlockSpec((1, ROWS // 2), lambda g: (0, 0)),
            pl.BlockSpec((ROWS, WIDE), lambda g: (0, g)),
            pl.BlockSpec((ROWS, GROUP * HEAD), lambda g: (0, g)),
            pl.BlockSpec((ROWS, GROUP * HEAD), lambda g: (0, g)),
        ],
        out_specs=(
            pl.BlockSpec((2, 2, 2, GROUP, 2, CHUNK, HEAD), lambda g: (0, 0, 0, g, 0, 0, 0)),
            pl.BlockSpec((ROWS, ROWS), lambda g: (0, 0)),
        ),
        out_shape=(
            jax.ShapeDtypeStruct((2, 2, 2, KEY_HEADS, 2, CHUNK, HEAD), BF16),
            jax.ShapeDtypeStruct((ROWS, ROWS), BF16),
        ),
        scratch_shapes=[pltpu.VMEM((ROWS, ROWS), BF16), pltpu.VMEM((INSTANCES, 8, ROWS), BF16)],
        compiler_params=ROOM,
        name="pack",
    )(facts, target, block, q, k, v)
    return rows.reshape(DEVICES, CHUNK, HEAD), place


def slot_positions(turn, rows_ref):
    label = rows_ref[:, SENT:CHUNK, :].astype(F32).reshape(DEVICES // 8, 8, 8, HEAD)
    label = jnp.sum(label, axis=1)
    row = lax.broadcasted_iota(jnp.int32, label.shape, 1)
    part = jnp.where(row == 2 * turn, label * 64.0, jnp.where(row == 2 * turn + 1, label, 0.0))
    return jnp.sum(part, axis=1) - 1.0


def line_up(pos):
    return jnp.concatenate([pos[j : j + 1] for j in range(DEVICES // 8)], axis=1)


def sorted_pair(line_ref, rows_refs, c):
    slots = DEVICES * CAP
    wanted = lax.broadcasted_iota(jnp.int32, (SORTED, slots), 0) + pl.program_id(0) * SORTED
    found = None
    for turn, rows_ref in enumerate(rows_refs):
        pick = jnp.where(line_ref[turn, 0:1, :] == wanted, 1.0, 0.0).astype(BF16)
        pair = [rows_ref[:, p * CAP : (p + 1) * CAP, :].reshape(slots, HEAD) for p in (c, c + 1)]
        added = jnp.dot(pick, jnp.concatenate(pair, axis=1), preferred_element_type=F32)
        found = added if found is None else found + added
    return found


def sort_keys_kernel(rounds, *refs):
    rows_refs = refs[:rounds]
    keys_ref, values_ref, line_ref, column_ref, most_ref = refs[rounds:]

    @pl.when(pl.program_id(0) == 0)
    def _():
        for turn in range(rounds):
            pos = slot_positions(turn, rows_refs[0])
            line_ref[turn] = jnp.broadcast_to(line_up(pos).astype(jnp.int32), (8, DEVICES * CAP))
            empty = jnp.zeros((HEAD - DEVICES // 8, HEAD), F32)
            column_ref[turn] = jnp.concatenate([pos, empty], axis=0).T
        count = rows_refs[0][:, SENT:CHUNK, :].astype(F32)
        row = lax.broadcasted_iota(jnp.int32, count.shape, 1)
        most_ref[0] = jnp.max(jnp.where(row == 4, count, 0.0)).astype(jnp.int32)

    found = sorted_pair(line_ref, rows_refs, 4)
    keys_ref[...] = found[:, :HEAD].astype(BF16)
    values_ref[...] = found[:, HEAD:].T.astype(BF16)


def sort_keys(rows):
    rounds, slots = len(rows), DEVICES * CAP
    line, column = (rounds, 8, slots), (rounds, HEAD, HEAD)
    return pl.pallas_call(
        functools.partial(sort_keys_kernel, rounds),
        grid=(SEQ_BLOCKS // SORTED,),
        in_specs=[pl.BlockSpec((DEVICES, CHUNK, HEAD), lambda t: (0, 0, 0))] * rounds,
        out_specs=(
            pl.BlockSpec((SORTED, HEAD), lambda t: (t, 0)),
            pl.BlockSpec((HEAD, SORTED), lambda t: (0, t)),
            pl.BlockSpec(line, lambda t: (0, 0, 0)),
            pl.BlockSpec(column, lambda t: (0, 0, 0)),
            pl.BlockSpec(memory_space=pltpu.SMEM),
        ),
        out_shape=(
            jax.ShapeDtypeStruct((SEQ_BLOCKS, HEAD), BF16),
            jax.ShapeDtypeStruct((HEAD, SEQ_BLOCKS), BF16),
            jax.ShapeDtypeStruct(line, jnp.int32),
            jax.ShapeDtypeStruct(column, F32),
            jax.ShapeDtypeStruct((1,), jnp.int32),
        ),
        compiler_params=ROOM,
        name="sort_keys",
    )(*rows)


def sort_queries_kernel(line_ref, *refs):
    out_ref = refs[-1]
    for c in range(0, 4, 2):
        found = sorted_pair(line_ref, refs[:-1], c).astype(BF16)
        out_ref[c] = found[:, :HEAD]
        out_ref[c + 1] = found[:, HEAD:]


def sort_queries(line, rows):
    flops = 2 * SEQ_BLOCKS * DEVICES * CAP * len(rows) * 4 * HEAD
    return pl.pallas_call(
        sort_queries_kernel,
        grid=(SEQ_BLOCKS // SORTED,),
        in_specs=[pl.BlockSpec(line.shape, lambda t: (0, 0, 0))]
        + [pl.BlockSpec((DEVICES, 4 * CAP, HEAD), lambda t: (0, 0, 0))] * len(rows),
        out_specs=pl.BlockSpec((4, SORTED, HEAD), lambda t: (0, t, 0)),
        out_shape=jax.ShapeDtypeStruct((4, SEQ_BLOCKS, HEAD), BF16),
        compiler_params=ROOM,
        cost_estimate=pl.CostEstimate(flops=flops, bytes_accessed=4 << 20, transcendentals=0),
        name="sort_queries",
    )(line, *rows)


def attend_tile(
    shift, tile, facts_ref, q_ref, own_keys, own_values, other_keys, other_values, out_ref, sum_ref, extra_ref
):
    core = facts_ref[0]
    span = 2 * TILE
    columns = 4 * TILE
    first = tile * span
    queries_ref = q_ref.at[:, pl.ds(pl.multiple_of(tile % TURNS * TILE, TILE), TILE), :]

    def start_of(position):
        start, end = jnp.zeros_like(position), jnp.int32(0)
        for d in range(2, facts_ref.shape[0]):
            end = end + facts_ref[d]
            start = jnp.where(end <= position, end, start)
        return start

    column = lax.broadcasted_iota(jnp.int32, (1, columns), 1)
    query_pos = first + (column % TILE) * 2 + column // (2 * TILE)
    query_start = start_of(query_pos)

    def key_pos(at, wide, index):
        own = index < wide * TILE
        block = jnp.where(own, index, index - wide * TILE) + at * TILE
        return block * 2 + jnp.where(own, core, 1 - core)

    def scores_of(at, wide):
        at_keys = pl.ds(pl.multiple_of(at * TILE, TILE), wide * TILE)
        keys = jnp.concatenate([own_keys[at_keys, :], other_keys[at_keys, :]], axis=0)
        scores = lax.dot_general(
            keys,
            queries_ref[...].reshape(columns, HEAD),
            (((1,), (1,)), ((), ())),
            preferred_element_type=F32,
        )
        return scores * SCALE

    def allowed_scores(at, whole):
        pos = key_pos(at, 1, lax.broadcasted_iota(jnp.int32, (span, 1), 0))
        allowed = (pos <= query_pos) & (pos >= query_start) if whole else pos <= query_pos
        return jnp.where(allowed, scores_of(at, 1), -1e30)

    def mixed(at, wide, weights, start=None):
        at_keys = pl.ds(pl.multiple_of(at * TILE, TILE), wide * TILE)
        values = jnp.concatenate([own_values[:, at_keys], other_values[:, at_keys]], axis=1)
        ones = jnp.ones((16, wide * span), BF16)
        if start is not None:
            pos = key_pos(at, wide, lax.broadcasted_iota(jnp.int32, (16, wide * span), 1))
            ones = jnp.where(pos >= start, 1.0, 0.0).astype(BF16)
            values = values * ones[0:1]
        values = jnp.concatenate([values, ones], axis=0)
        return jnp.dot(values, weights.astype(BF16), preferred_element_type=F32)

    start = start_of(first)
    low = start // span

    if shift:

        def shifted(at, begins):
            scores = allowed_scores(at, True)
            best = jnp.broadcast_to(jnp.max(scores, axis=0, keepdims=True), (8, columns))
            top = best if begins else jnp.maximum(extra_ref[...], best)
            added = mixed(at, 1, jnp.exp2(scores - top[0:1]))
            if begins:
                sum_ref[...] = added
            else:
                sum_ref[...] = sum_ref[...] * jnp.exp2(extra_ref[0:1] - top[0:1]) + added
            extra_ref[...] = top

        shifted(tile, True)

        @pl.loop(low, tile)
        def _(at):
            shifted(at, False)

    else:
        sum_ref[...] = jnp.zeros_like(sum_ref)
        left = tile - low
        for wide in (1, 2, 4):

            @pl.when((left // wide) % 2 == 1)
            def _():
                at = low + left % wide
                sum_ref[...] += mixed(at, wide, jnp.exp2(scores_of(at, wide)), start)

        split = start_of(first + span - 1) > first

        @pl.when(split)
        def _():
            added = mixed(tile, 1, jnp.exp2(allowed_scores(tile, True)))
            sum_ref[...] = jnp.where(query_start <= first, sum_ref[...], 0.0) + added

        @pl.when(jnp.logical_not(split))
        def _():
            sum_ref[...] += mixed(tile, 1, jnp.exp2(allowed_scores(tile, False)))

        total = sum_ref[HEAD : HEAD + 8]
        extra_ref[...] += jnp.where((total <= 2.0**100) & (total >= 2.0**-80), 0.0, 1.0)

    done = (sum_ref[:HEAD] / sum_ref[HEAD : HEAD + 1]).astype(BF16)
    place = pl.ds(pl.multiple_of(tile * TILE, TILE), TILE)
    for c in range(4):
        out_ref[c * HEAD : (c + 1) * HEAD, place] = done[:, c * TILE : (c + 1) * TILE]


def unsort_tile(step, column_ref, attended_ref, out_ref):
    lane = lax.broadcasted_iota(jnp.int32, (HEAD, HEAD), 1)
    turn, near = step // UNSORTS, step % UNSORTS
    wide = UNSORTED // HEAD
    columns = [
        jnp.sum(jnp.where(lane == near * wide + j, column_ref[turn], 0.0), axis=1, keepdims=True)
        for j in range(wide)
    ]
    pos = jnp.concatenate(columns, axis=0).astype(jnp.int32)
    block = lax.broadcasted_iota(jnp.int32, (UNSORTED, SEQ_BLOCKS), 1)
    pick = jnp.where(pos == block, 1.0, 0.0).astype(BF16)
    for c in range(0, 4, 2):
        found = lax.dot_general(
            pick,
            attended_ref[c * HEAD : (c + 2) * HEAD, :],
            (((1,), (1,)), ((), ())),
            preferred_element_type=F32,
        ).astype(BF16)
        for p in range(2):
            part = found[:, p * HEAD : (p + 1) * HEAD].reshape(UNSORTED // CAP, CAP, HEAD)
            out_ref[:, (c + p) * CAP : (c + p + 1) * CAP, :] = part


def attend_kernel(facts_ref, column_ref, q_ref, *refs):
    key_refs, out_ref, attended_ref, more = refs[:4], refs[4], refs[5], refs[6:]
    step = pl.program_id(0)

    def attend_tiles(shift):
        @pl.loop(step * TURNS, (step + 1) * TURNS)
        def _(tile):
            attend_tile(shift, tile, facts_ref, q_ref, *key_refs, attended_ref, *more)

    @pl.when(step < TILES // TURNS)
    def _():
        extra_ref = more[1]
        extra_ref[...] = jnp.zeros_like(extra_ref)
        attend_tiles(False)

        @pl.when(jnp.max(extra_ref[...]) > 0.0)
        def _():
            attend_tiles(True)

    @pl.when(step >= TILES // TURNS)
    def _():
        unsort_tile(step - TILES // TURNS, column_ref, attended_ref, out_ref)


def attend(facts, column, queries, own, other):
    rounds, steps = column.shape[0], TILES // TURNS
    keys = pl.BlockSpec((SEQ_BLOCKS, HEAD), lambda t: (0, 0))
    values = pl.BlockSpec((HEAD, SEQ_BLOCKS), lambda t: (0, 0))
    return pl.pallas_call(
        attend_kernel,
        grid=(steps + rounds * UNSORTS,),
        in_specs=[
            pl.BlockSpec(memory_space=pltpu.SMEM),
            pl.BlockSpec(column.shape, lambda t: (0, 0, 0)),
            pl.BlockSpec((4, TURNS * TILE, HEAD), lambda t: (0, jnp.minimum(t, steps - 1), 0)),
            keys,
            values,
            keys,
            values,
        ],
        out_specs=pl.BlockSpec(
            (UNSORTED // CAP, BACK, HEAD), lambda t: (jnp.maximum(t - steps, 0), 0, 0)
        ),
        out_shape=jax.ShapeDtypeStruct((rounds * DEVICES, BACK, HEAD), BF16),
        scratch_shapes=[
            pltpu.VMEM((4 * HEAD, SEQ_BLOCKS), BF16),
            pltpu.VMEM((HEAD + 16, 4 * TILE), F32),
            pltpu.VMEM((8, 4 * TILE), F32),
        ],
        compiler_params=ROOM,
        name="attend",
    )(facts, column, queries, *own, *other)


def unpack_kernel(rounds, *refs):
    place_refs, back_refs, out_ref = refs[:rounds], refs[rounds:-1], refs[-1]
    total = jnp.zeros(out_ref.shape, F32)
    for turn in range(rounds):
        lines = []
        for parity in range(2):
            for i in range(INSTANCES):
                line = []
                for g in range(GROUP):
                    for r in range(4):
                        of = (i // 2, r % 2, i % 2, g, r // 2)
                        for h in range(2):
                            at = (2 * parity + h) * CAP
                            line.append(back_refs[turn][(*of, slice(at, at + CAP), slice(None))])
                lines.append(jnp.concatenate(line, axis=1))
        total = total + jnp.dot(
            place_refs[turn][...], jnp.concatenate(lines, axis=0), preferred_element_type=F32
        )
    out_ref[...] = total.astype(BF16)


def unpack(places, backs):
    rounds = len(backs)
    block = pl.BlockSpec((2, 2, 2, GROUP, 2, BACK, HEAD), lambda g: (0, 0, 0, g, 0, 0, 0))
    return pl.pallas_call(
        functools.partial(unpack_kernel, rounds),
        grid=(KEY_HEADS // GROUP,),
        in_specs=[pl.BlockSpec((ROWS, ROWS), lambda g: (0, 0))] * rounds + [block] * rounds,
        out_specs=pl.BlockSpec((ROWS, WIDE), lambda g: (0, g)),
        out_shape=jax.ShapeDtypeStruct((ROWS, KEY_HEADS * 8 * HEAD), BF16),
        compiler_params=ROOM,
        name="unpack",
    )(*places, *(b.reshape(2, 2, 2, KEY_HEADS, 2, BACK, HEAD) for b in backs))


def exchange(x):
    return lax.all_to_all(x, BOTH, split_axis=0, concat_axis=0, tiled=True)


def shards(query_rows, key_rows, value_rows, target_instance, block_position, request_lengths):
    spot, place = lax.axis_index("inst"), lax.axis_index("seq")
    core = spot % 2
    instance = (spot // 2) * 2 + place // 16
    lengths = lax.dynamic_index_in_dim(request_lengths, instance, 0, keepdims=False)
    facts = jnp.concatenate([jnp.stack([core, (place % 8) * CAP]), lengths]).astype(jnp.int32)
    plan = (facts, target_instance[None, :], block_position[None, :])

    def run(rounds):
        packed = [pack(t, *plan, query_rows, key_rows, value_rows) for t in range(rounds)]
        rows = [exchange(sent) for sent, _ in packed]
        keys, values, line, column, most = sort_keys(rows)
        pairs = [(0, 1), (1, 0), (2, 3), (3, 2)]
        other = [lax.ppermute(x, "inst", pairs) for x in (keys, values)]
        back = attend(facts, column, sort_queries(line, rows), (keys, values), other)
        backs = [exchange(back[t * DEVICES : (t + 1) * DEVICES]) for t in range(rounds)]
        return unpack([places for _, places in packed], backs), most[0]

    attended, most = run(1)
    return lax.while_loop(
        lambda state: state[1] > CAP,
        lambda state: (run(2)[0], jnp.zeros_like(state[1])),
        (attended, most),
    )[0]


def solution(mesh):
    rows = P(BOTH, None)
    return jax.shard_map(
        shards,
        mesh=mesh,
        in_specs=(rows, rows, rows, P(BOTH), P(BOTH), P()),
        out_specs=rows,
        check_vma=False,
    )
```

```python
import functools
import math

import jax
import jax.numpy as jnp
from jax import lax
from jax.experimental import pallas as pl
from jax.experimental.pallas import tpu as pltpu
from jax.sharding import PartitionSpec as P

BOTH = ("inst", "seq")
INSTANCES = 4
DEVICES = 128
KEY_HEADS = 8
HEAD = 128
ROWS = 128
CAP = 16
SLOTS = INSTANCES * CAP
SEQ_BLOCKS = 2048
TILE = 256
TILES = SEQ_BLOCKS // TILE
SORTED = 1024
UNSORTED = 512
UNSORTS = DEVICES * CAP // UNSORTED
SENT = 6 * CAP
CHUNK = SENT + 8
BACK = 4 * CAP
GROUP = 4
WIDE = GROUP * 8 * HEAD
SCALE = math.log2(math.e) / math.sqrt(HEAD)
HERE = pl.BlockSpec(memory_space=pltpu.VMEM)
NEAR = pl.BlockSpec(memory_space=pltpu.SMEM)
ROOM = pltpu.CompilerParams(vmem_limit_bytes=28 << 20)
F32 = jnp.float32
BF16 = jnp.bfloat16


def plan_pack(turn, offset_ref, target_ref, block_ref, pick_ref, label_ref, place_ref):
    shape = (ROWS, ROWS)
    half = jnp.full((1, ROWS // 2), -1.0, F32)
    inst_l = jnp.concatenate([target_ref[...].astype(F32), half], axis=1)
    pos_l = jnp.concatenate([block_ref[...].astype(F32), half], axis=1)
    inst_s, pos_s = jnp.broadcast_to(inst_l, shape).T, jnp.broadcast_to(pos_l, shape).T
    lane = lax.broadcasted_iota(jnp.int32, shape, 1)
    sub = lax.broadcasted_iota(jnp.int32, shape, 0)
    ahead = (inst_l == inst_s) & (pos_l < pos_s)
    rank = jnp.sum(jnp.where(ahead, 1.0, 0.0), axis=1, keepdims=True)
    step = rank - turn * CAP
    slot = jnp.where((step >= 0) & (step < CAP), inst_s * CAP + step, -1.0)
    slot = jnp.sum(jnp.where(lane // 2 == sub, slot, 0.0), axis=0, keepdims=True)
    hit = (slot == (sub % SLOTS).astype(F32)) & (lane % 2 == sub // SLOTS)
    pick = jnp.where(hit, 1.0, 0.0)
    pick_ref[...] = pick.astype(BF16)
    place_ref[...] = pick.T.astype(BF16)
    most = jnp.max(jnp.broadcast_to(rank, shape), axis=0, keepdims=True) + 1.0
    row = sub[:8]
    at = lane - offset_ref[0]
    for i in range(INSTANCES):
        label = jnp.where(row == 4, most, 0.0)
        for t in range(2):
            here = (inst_s == i) & (rank == (at + t * CAP).astype(F32)) & (at >= 0) & (at < CAP)
            block = jnp.sum(jnp.where(here, pos_s + 1.0, 0.0), axis=0, keepdims=True)
            high = jnp.floor(block * (1.0 / 64.0))
            label = jnp.where(row == 2 * t, high, label)
            label = jnp.where(row == 2 * t + 1, block - high * 64.0, label)
        label_ref[i] = label.astype(BF16)


def pack_kernel(turn, offset_ref, target_ref, block_ref, q_ref, k_ref, v_ref, out_ref, place_ref, pick_ref, label_ref):
    @pl.when(pl.program_id(0) == 0)
    def _():
        plan_pack(turn, offset_ref, target_ref, block_ref, pick_ref, label_ref, place_ref)

    pick = pick_ref[...]
    queries = jnp.dot(pick, q_ref[...], preferred_element_type=F32).astype(BF16)
    keys = jnp.dot(pick, k_ref[...], preferred_element_type=F32).astype(BF16)
    values = jnp.dot(pick, v_ref[...], preferred_element_type=F32).astype(BF16)
    for i in range(INSTANCES):
        for g in range(GROUP):
            for r in range(4):
                to = (i // 2, r % 2, i % 2, g, r // 2)
                for c in range(4):
                    at = (c // 2) * SLOTS + i * CAP
                    head = (8 * g + 2 * r + c % 2) * HEAD
                    out_ref[(*to, slice(c * CAP, (c + 1) * CAP), slice(None))] = queries[
                        at : at + CAP, head : head + HEAD
                    ]
                at = (r % 2) * SLOTS + i * CAP
                lanes = slice(g * HEAD, (g + 1) * HEAD)
                out_ref[(*to, slice(4 * CAP, 5 * CAP), slice(None))] = keys[at : at + CAP, lanes]
                out_ref[(*to, slice(5 * CAP, 6 * CAP), slice(None))] = values[at : at + CAP, lanes]
                out_ref[(*to, slice(SENT, CHUNK), slice(None))] = label_ref[i]


def pack(turn, offset, target, block, q, k, v):
    rows, place = pl.pallas_call(
        functools.partial(pack_kernel, turn),
        grid=(KEY_HEADS // GROUP,),
        in_specs=[
            NEAR,
            pl.BlockSpec((1, ROWS // 2), lambda g: (0, 0)),
            pl.BlockSpec((1, ROWS // 2), lambda g: (0, 0)),
            pl.BlockSpec((ROWS, WIDE), lambda g: (0, g)),
            pl.BlockSpec((ROWS, GROUP * HEAD), lambda g: (0, g)),
            pl.BlockSpec((ROWS, GROUP * HEAD), lambda g: (0, g)),
        ],
        out_specs=(
            pl.BlockSpec((2, 2, 2, GROUP, 2, CHUNK, HEAD), lambda g: (0, 0, 0, g, 0, 0, 0)),
            pl.BlockSpec((ROWS, ROWS), lambda g: (0, 0)),
        ),
        out_shape=(
            jax.ShapeDtypeStruct((2, 2, 2, KEY_HEADS, 2, CHUNK, HEAD), BF16),
            jax.ShapeDtypeStruct((ROWS, ROWS), BF16),
        ),
        scratch_shapes=[pltpu.VMEM((ROWS, ROWS), BF16), pltpu.VMEM((INSTANCES, 8, ROWS), BF16)],
        compiler_params=ROOM,
        name="pack",
    )(offset, target, block, q, k, v)
    return rows.reshape(DEVICES, CHUNK, HEAD), place


def slot_positions(turn, rows_ref):
    label = rows_ref[:, SENT:CHUNK, :].astype(F32).reshape(DEVICES // 8, 8, 8, HEAD)
    label = jnp.sum(label, axis=1)
    row = lax.broadcasted_iota(jnp.int32, label.shape, 1)
    part = jnp.where(row == 2 * turn, label * 64.0, jnp.where(row == 2 * turn + 1, label, 0.0))
    return jnp.sum(part, axis=1) - 1.0


def line_up(pos):
    return jnp.concatenate([pos[j : j + 1] for j in range(DEVICES // 8)], axis=1).astype(jnp.int32)


def sorted_pair(first, lines, rows_refs, c):
    slots = DEVICES * CAP
    wanted = lax.broadcasted_iota(jnp.int32, (SORTED, slots), 0) + first
    found = None
    for turn, rows_ref in enumerate(rows_refs):
        pick = jnp.where(lines[turn] == wanted, 1.0, 0.0).astype(BF16)
        pair = [rows_ref[:, p * CAP : (p + 1) * CAP, :].reshape(slots, HEAD) for p in (c, c + 1)]
        added = jnp.dot(pick, jnp.concatenate(pair, axis=1), preferred_element_type=F32)
        found = added if found is None else found + added
    return found


def sort_keys_kernel(rounds, *refs):
    rows_refs = refs[:rounds]
    keys_ref, values_ref, column_ref, most_ref = refs[rounds:]
    lines = []
    for turn in range(rounds):
        pos = slot_positions(turn, rows_refs[0])
        lines.append(line_up(pos))
        empty = jnp.zeros((HEAD - DEVICES // 8, HEAD), F32)
        column_ref[turn] = jnp.concatenate([pos, empty], axis=0).T
    count = rows_refs[0][:, SENT:CHUNK, :].astype(F32)
    row = lax.broadcasted_iota(jnp.int32, count.shape, 1)
    most_ref[0] = jnp.max(jnp.where(row == 4, count, 0.0)).astype(jnp.int32)
    for first in range(0, SEQ_BLOCKS, SORTED):
        found = sorted_pair(first, lines, rows_refs, 4)
        keys_ref[first : first + SORTED] = found[:, :HEAD].astype(BF16)
        values_ref[:, first : first + SORTED] = found[:, HEAD:].T.astype(BF16)


def sort_keys(rows):
    rounds = len(rows)
    return pl.pallas_call(
        functools.partial(sort_keys_kernel, rounds),
        in_specs=[HERE] * rounds,
        out_specs=(HERE, HERE, HERE, NEAR),
        out_shape=(
            jax.ShapeDtypeStruct((SEQ_BLOCKS, HEAD), BF16),
            jax.ShapeDtypeStruct((HEAD, SEQ_BLOCKS), BF16),
            jax.ShapeDtypeStruct((rounds, HEAD, HEAD), F32),
            jax.ShapeDtypeStruct((1,), jnp.int32),
        ),
        compiler_params=ROOM,
        name="sort_keys",
    )(*rows)


def sort_queries_kernel(*refs):
    rows_refs, out_ref = refs[:-1], refs[-1]
    lines = [line_up(slot_positions(turn, rows_refs[0])) for turn in range(len(rows_refs))]
    for first in range(0, SEQ_BLOCKS, SORTED):
        for c in range(0, 4, 2):
            found = sorted_pair(first, lines, rows_refs, c).astype(BF16)
            out_ref[c, first : first + SORTED] = found[:, :HEAD]
            out_ref[c + 1, first : first + SORTED] = found[:, HEAD:]


def sort_queries(rows):
    flops = 2 * SEQ_BLOCKS * DEVICES * CAP * len(rows) * 4 * HEAD
    return pl.pallas_call(
        sort_queries_kernel,
        in_specs=[HERE] * len(rows),
        out_specs=HERE,
        out_shape=jax.ShapeDtypeStruct((4, SEQ_BLOCKS, HEAD), BF16),
        compiler_params=ROOM,
        cost_estimate=pl.CostEstimate(flops=flops, bytes_accessed=4 << 20, transcendentals=0),
        name="sort_queries",
    )(*rows)


def attend_tile(
    shift, tile, facts_ref, q_ref, own_keys, own_values, other_keys, other_values, out_ref, sum_ref, extra_ref
):
    core = facts_ref[0]
    span = 2 * TILE
    columns = 4 * TILE
    first = tile * span
    queries_ref = q_ref.at[:, pl.ds(pl.multiple_of(tile * TILE, TILE), TILE), :]

    def start_of(position):
        start, end = jnp.zeros_like(position), jnp.int32(0)
        for d in range(1, facts_ref.shape[0]):
            end = end + facts_ref[d]
            start = jnp.where(end <= position, end, start)
        return start

    column = lax.broadcasted_iota(jnp.int32, (1, columns), 1)
    query_pos = first + (column % TILE) * 2 + column // (2 * TILE)
    query_start = start_of(query_pos)

    def key_pos(at, wide, index):
        own = index < wide * TILE
        block = jnp.where(own, index, index - wide * TILE) + at * TILE
        return block * 2 + jnp.where(own, core, 1 - core)

    def scores_of(at, wide):
        at_keys = pl.ds(pl.multiple_of(at * TILE, TILE), wide * TILE)
        keys = jnp.concatenate([own_keys[at_keys, :], other_keys[at_keys, :]], axis=0)
        scores = lax.dot_general(
            keys,
            queries_ref[...].reshape(columns, HEAD),
            (((1,), (1,)), ((), ())),
            preferred_element_type=F32,
        )
        return scores * SCALE

    def allowed_scores(at, whole):
        pos = key_pos(at, 1, lax.broadcasted_iota(jnp.int32, (span, 1), 0))
        allowed = (pos <= query_pos) & (pos >= query_start) if whole else pos <= query_pos
        return jnp.where(allowed, scores_of(at, 1), -1e30)

    def mixed(at, wide, weights, start=None):
        at_keys = pl.ds(pl.multiple_of(at * TILE, TILE), wide * TILE)
        values = jnp.concatenate([own_values[:, at_keys], other_values[:, at_keys]], axis=1)
        ones = jnp.ones((16, wide * span), BF16)
        if start is not None:
            pos = key_pos(at, wide, lax.broadcasted_iota(jnp.int32, (16, wide * span), 1))
            ones = jnp.where(pos >= start, 1.0, 0.0).astype(BF16)
            values = values * ones[0:1]
        values = jnp.concatenate([values, ones], axis=0)
        return jnp.dot(values, weights.astype(BF16), preferred_element_type=F32)

    start = start_of(first)
    low = start // span

    if shift:

        def shifted(at, begins):
            scores = allowed_scores(at, True)
            best = jnp.broadcast_to(jnp.max(scores, axis=0, keepdims=True), (8, columns))
            top = best if begins else jnp.maximum(extra_ref[...], best)
            added = mixed(at, 1, jnp.exp2(scores - top[0:1]))
            if begins:
                sum_ref[...] = added
            else:
                sum_ref[...] = sum_ref[...] * jnp.exp2(extra_ref[0:1] - top[0:1]) + added
            extra_ref[...] = top

        shifted(tile, True)

        @pl.loop(low, tile)
        def _(at):
            shifted(at, False)

    else:
        split = start_of(first + span - 1) > first

        @pl.when(split)
        def _():
            sum_ref[...] = mixed(tile, 1, jnp.exp2(allowed_scores(tile, True)))

        @pl.when(jnp.logical_not(split))
        def _():
            sum_ref[...] = mixed(tile, 1, jnp.exp2(allowed_scores(tile, False)))

        left = tile - low
        for wide in (1, 2, 4):

            @pl.when((left // wide) % 2 == 1)
            def _():
                at = low + left % wide
                added = mixed(at, wide, jnp.exp2(scores_of(at, wide)), start)
                sum_ref[...] += jnp.where(query_start <= first, added, 0.0)

        total = sum_ref[HEAD : HEAD + 8]
        extra_ref[...] += jnp.where((total <= 2.0**100) & (total >= 2.0**-80), 0.0, 1.0)

    done = (sum_ref[:HEAD] * (1.0 / sum_ref[HEAD : HEAD + 8])[0:1]).astype(BF16)
    place = pl.ds(pl.multiple_of(tile * TILE, TILE), TILE)
    for c in range(4):
        out_ref[c * HEAD : (c + 1) * HEAD, place] = done[:, c * TILE : (c + 1) * TILE]


def unsort_tile(turn, near, column_ref, attended_ref, out_ref):
    lane = lax.broadcasted_iota(jnp.int32, (HEAD, HEAD), 1)
    wide = UNSORTED // HEAD
    columns = [
        jnp.sum(jnp.where(lane == near * wide + j, column_ref[turn], 0.0), axis=1, keepdims=True)
        for j in range(wide)
    ]
    pos = jnp.concatenate(columns, axis=0).astype(jnp.int32)
    block = lax.broadcasted_iota(jnp.int32, (UNSORTED, SEQ_BLOCKS), 1)
    pick = jnp.where(pos == block, 1.0, 0.0).astype(BF16)
    for c in range(0, 4, 2):
        found = lax.dot_general(
            pick,
            attended_ref[c * HEAD : (c + 2) * HEAD, :],
            (((1,), (1,)), ((), ())),
            preferred_element_type=F32,
        ).astype(BF16)
        for p in range(2):
            part = found[:, p * HEAD : (p + 1) * HEAD].reshape(UNSORTED // CAP, CAP, HEAD)
            devices = slice((turn * UNSORTS + near) * UNSORTED // CAP, (turn * UNSORTS + near + 1) * UNSORTED // CAP)
            out_ref[devices, (c + p) * CAP : (c + p + 1) * CAP, :] = part


def attend_kernel(facts_ref, column_ref, q_ref, *refs):
    key_refs, out_ref, attended_ref, more = refs[:4], refs[4], refs[5], refs[6:]

    def attend_tiles(shift):
        @pl.loop(0, TILES)
        def _(tile):
            attend_tile(shift, tile, facts_ref, q_ref, *key_refs, attended_ref, *more)

    extra_ref = more[1]
    extra_ref[...] = jnp.zeros_like(extra_ref)
    attend_tiles(False)

    @pl.when(jnp.max(extra_ref[...]) > 0.0)
    def _():
        attend_tiles(True)

    for turn in range(column_ref.shape[0]):
        for near in range(UNSORTS):
            unsort_tile(turn, near, column_ref, attended_ref, out_ref)


def attend(facts, column, queries, own, other):
    return pl.pallas_call(
        attend_kernel,
        in_specs=[NEAR] + [HERE] * 6,
        out_specs=HERE,
        out_shape=jax.ShapeDtypeStruct((column.shape[0] * DEVICES, BACK, HEAD), BF16),
        scratch_shapes=[
            pltpu.VMEM((4 * HEAD, SEQ_BLOCKS), BF16),
            pltpu.VMEM((HEAD + 16, 4 * TILE), F32),
            pltpu.VMEM((8, 4 * TILE), F32),
        ],
        compiler_params=ROOM,
        name="attend",
    )(facts, column, queries, *own, *other)


def unpack_kernel(rounds, *refs):
    place_refs, back_refs, out_ref = refs[:rounds], refs[rounds:-1], refs[-1]
    total = jnp.zeros(out_ref.shape, F32)
    for turn in range(rounds):
        lines = []
        for parity in range(2):
            for i in range(INSTANCES):
                line = []
                for g in range(GROUP):
                    for r in range(4):
                        of = (i // 2, r % 2, i % 2, g, r // 2)
                        for h in range(2):
                            at = (2 * parity + h) * CAP
                            line.append(back_refs[turn][(*of, slice(at, at + CAP), slice(None))])
                lines.append(jnp.concatenate(line, axis=1))
        total = total + jnp.dot(
            place_refs[turn][...], jnp.concatenate(lines, axis=0), preferred_element_type=F32
        )
    out_ref[...] = total.astype(BF16)


def unpack(places, backs):
    rounds = len(backs)
    block = pl.BlockSpec((2, 2, 2, GROUP, 2, BACK, HEAD), lambda g: (0, 0, 0, g, 0, 0, 0))
    return pl.pallas_call(
        functools.partial(unpack_kernel, rounds),
        grid=(KEY_HEADS // GROUP,),
        in_specs=[pl.BlockSpec((ROWS, ROWS), lambda g: (0, 0))] * rounds + [block] * rounds,
        out_specs=pl.BlockSpec((ROWS, WIDE), lambda g: (0, g)),
        out_shape=jax.ShapeDtypeStruct((ROWS, KEY_HEADS * 8 * HEAD), BF16),
        compiler_params=ROOM,
        name="unpack",
    )(*places, *(b.reshape(2, 2, 2, KEY_HEADS, 2, BACK, HEAD) for b in backs))


def exchange(x):
    return lax.all_to_all(x, BOTH, split_axis=0, concat_axis=0, tiled=True)


def shards(query_rows, key_rows, value_rows, target_instance, block_position, request_lengths):
    spot, place = lax.axis_index("inst"), lax.axis_index("seq")
    core = spot % 2
    instance = (spot // 2) * 2 + place // 16
    lengths = lax.dynamic_index_in_dim(request_lengths, instance, 0, keepdims=False)
    facts = jnp.concatenate([core[None], lengths]).astype(jnp.int32)
    plan = ((place % 8 * CAP)[None], target_instance[None, :], block_position[None, :])

    def run(rounds):
        packed = [pack(t, *plan, query_rows, key_rows, value_rows) for t in range(rounds)]
        rows = [exchange(sent) for sent, _ in packed]
        keys, values, column, most = sort_keys(rows)
        pairs = [(0, 1), (1, 0), (2, 3), (3, 2)]
        other = [lax.ppermute(x, "inst", pairs) for x in (keys, values)]
        back = attend(facts, column, sort_queries(rows), (keys, values), other)
        backs = [exchange(back[t * DEVICES : (t + 1) * DEVICES]) for t in range(rounds)]
        return unpack([places for _, places in packed], backs), most[0]

    attended, most = run(1)
    return lax.while_loop(
        lambda state: state[1] > CAP,
        lambda state: (run(2)[0], jnp.zeros_like(state[1])),
        (attended, most),
    )[0]


def solution(mesh):
    rows = P(BOTH, None)
    return jax.shard_map(
        shards,
        mesh=mesh,
        in_specs=(rows, rows, rows, P(BOTH), P(BOTH), P()),
        out_specs=rows,
        check_vma=False,
    )
```

```python
import functools
import math

import jax
import jax.numpy as jnp
from jax import lax
from jax.experimental import pallas as pl
from jax.experimental.pallas import tpu as pltpu
from jax.sharding import PartitionSpec as P

BOTH = ("inst", "seq")
INSTANCES = 4
DEVICES = 128
KEY_HEADS = 8
HEAD = 128
ROWS = 128
CAP = 16
SLOTS = INSTANCES * CAP
SEQ_BLOCKS = 2048
TILE = 256
TILES = SEQ_BLOCKS // TILE
SORTED = 1024
UNSORTED = 512
UNSORTS = DEVICES * CAP // UNSORTED
SENT = 6 * CAP
CHUNK = SENT + 8
BACK = 4 * CAP
GROUP = 4
WIDE = GROUP * 8 * HEAD
SCALE = math.log2(math.e) / math.sqrt(HEAD)
HERE = pl.BlockSpec(memory_space=pltpu.VMEM)
NEAR = pl.BlockSpec(memory_space=pltpu.SMEM)
ROOM = pltpu.CompilerParams(vmem_limit_bytes=28 << 20)
F32 = jnp.float32
BF16 = jnp.bfloat16


def plan_pack(turn, offset_ref, target_ref, block_ref, pick_ref, label_ref, place_ref):
    shape = (ROWS, ROWS)
    half = jnp.full((1, ROWS // 2), -1.0, F32)
    inst_l = jnp.concatenate([target_ref[...].astype(F32), half], axis=1)
    pos_l = jnp.concatenate([block_ref[...].astype(F32), half], axis=1)
    inst_s, pos_s = jnp.broadcast_to(inst_l, shape).T, jnp.broadcast_to(pos_l, shape).T
    lane = lax.broadcasted_iota(jnp.int32, shape, 1)
    sub = lax.broadcasted_iota(jnp.int32, shape, 0)
    ahead = (inst_l == inst_s) & (pos_l < pos_s)
    rank = jnp.sum(jnp.where(ahead, 1.0, 0.0), axis=1, keepdims=True)
    step = rank - turn * CAP
    slot = jnp.where((step >= 0) & (step < CAP), inst_s * CAP + step, -1.0)
    slot = jnp.sum(jnp.where(lane // 2 == sub, slot, 0.0), axis=0, keepdims=True)
    hit = (slot == (sub % SLOTS).astype(F32)) & (lane % 2 == sub // SLOTS)
    pick = jnp.where(hit, 1.0, 0.0)
    pick_ref[...] = pick.astype(BF16)
    place_ref[...] = pick.T.astype(BF16)
    most = jnp.max(jnp.broadcast_to(rank, shape), axis=0, keepdims=True) + 1.0
    row = sub[:8]
    at = lane - offset_ref[0]
    for i in range(INSTANCES):
        label = jnp.where(row == 4, most, 0.0)
        for t in range(2):
            here = (inst_s == i) & (rank == (at + t * CAP).astype(F32)) & (at >= 0) & (at < CAP)
            block = jnp.sum(jnp.where(here, pos_s + 1.0, 0.0), axis=0, keepdims=True)
            high = jnp.floor(block * (1.0 / 64.0))
            label = jnp.where(row == 2 * t, high, label)
            label = jnp.where(row == 2 * t + 1, block - high * 64.0, label)
        label_ref[i] = label.astype(BF16)


def pack_kernel(turn, offset_ref, target_ref, block_ref, q_ref, k_ref, v_ref, out_ref, place_ref, pick_ref, label_ref):
    @pl.when(pl.program_id(0) == 0)
    def _():
        plan_pack(turn, offset_ref, target_ref, block_ref, pick_ref, label_ref, place_ref)

    pick = pick_ref[...]
    queries = jnp.dot(pick, q_ref[...], preferred_element_type=F32).astype(BF16)
    keys = jnp.dot(pick, k_ref[...], preferred_element_type=F32).astype(BF16)
    values = jnp.dot(pick, v_ref[...], preferred_element_type=F32).astype(BF16)
    for i in range(INSTANCES):
        for g in range(GROUP):
            for r in range(4):
                to = (i // 2, r % 2, i % 2, g, r // 2)
                for c in range(4):
                    at = (c // 2) * SLOTS + i * CAP
                    head = (8 * g + 2 * r + c % 2) * HEAD
                    out_ref[(*to, slice(c * CAP, (c + 1) * CAP), slice(None))] = queries[
                        at : at + CAP, head : head + HEAD
                    ]
                at = (r % 2) * SLOTS + i * CAP
                lanes = slice(g * HEAD, (g + 1) * HEAD)
                out_ref[(*to, slice(4 * CAP, 5 * CAP), slice(None))] = keys[at : at + CAP, lanes]
                out_ref[(*to, slice(5 * CAP, 6 * CAP), slice(None))] = values[at : at + CAP, lanes]
                out_ref[(*to, slice(SENT, CHUNK), slice(None))] = label_ref[i]


def pack(turn, offset, target, block, q, k, v):
    rows, place = pl.pallas_call(
        functools.partial(pack_kernel, turn),
        grid=(KEY_HEADS // GROUP,),
        in_specs=[
            NEAR,
            pl.BlockSpec((1, ROWS // 2), lambda g: (0, 0)),
            pl.BlockSpec((1, ROWS // 2), lambda g: (0, 0)),
            pl.BlockSpec((ROWS, WIDE), lambda g: (0, g)),
            pl.BlockSpec((ROWS, GROUP * HEAD), lambda g: (0, g)),
            pl.BlockSpec((ROWS, GROUP * HEAD), lambda g: (0, g)),
        ],
        out_specs=(
            pl.BlockSpec((2, 2, 2, GROUP, 2, CHUNK, HEAD), lambda g: (0, 0, 0, g, 0, 0, 0)),
            pl.BlockSpec((ROWS, ROWS), lambda g: (0, 0)),
        ),
        out_shape=(
            jax.ShapeDtypeStruct((2, 2, 2, KEY_HEADS, 2, CHUNK, HEAD), BF16),
            jax.ShapeDtypeStruct((ROWS, ROWS), BF16),
        ),
        scratch_shapes=[pltpu.VMEM((ROWS, ROWS), BF16), pltpu.VMEM((INSTANCES, 8, ROWS), BF16)],
        compiler_params=ROOM,
        name="pack",
    )(offset, target, block, q, k, v)
    return rows.reshape(DEVICES, CHUNK, HEAD), place


def slot_positions(turn, rows_ref):
    label = rows_ref[:, SENT:CHUNK, :].astype(F32).reshape(DEVICES // 8, 8, 8, HEAD)
    label = jnp.sum(label, axis=1)
    row = lax.broadcasted_iota(jnp.int32, label.shape, 1)
    part = jnp.where(row == 2 * turn, label * 64.0, jnp.where(row == 2 * turn + 1, label, 0.0))
    return jnp.sum(part, axis=1) - 1.0


def line_up(pos):
    return jnp.concatenate([pos[j : j + 1] for j in range(DEVICES // 8)], axis=1).astype(jnp.int32)


def sorted_pair(first, lines, rows_refs, c):
    slots = DEVICES * CAP
    wanted = lax.broadcasted_iota(jnp.int32, (SORTED, slots), 0) + first
    found = None
    for turn, rows_ref in enumerate(rows_refs):
        pick = jnp.where(lines[turn] == wanted, 1.0, 0.0).astype(BF16)
        pair = [rows_ref[:, p * CAP : (p + 1) * CAP, :].reshape(slots, HEAD) for p in (c, c + 1)]
        added = jnp.dot(pick, jnp.concatenate(pair, axis=1), preferred_element_type=F32)
        found = added if found is None else found + added
    return found


def sort_keys_kernel(rounds, *refs):
    rows_refs = refs[:rounds]
    keys_ref, values_ref, column_ref, most_ref = refs[rounds:]
    lines = []
    for turn in range(rounds):
        pos = slot_positions(turn, rows_refs[0])
        lines.append(line_up(pos))
        empty = jnp.zeros((HEAD - DEVICES // 8, HEAD), F32)
        column_ref[turn] = jnp.concatenate([pos, empty], axis=0).T
    count = rows_refs[0][:, SENT:CHUNK, :].astype(F32)
    row = lax.broadcasted_iota(jnp.int32, count.shape, 1)
    most_ref[0] = jnp.max(jnp.where(row == 4, count, 0.0)).astype(jnp.int32)
    for first in range(0, SEQ_BLOCKS, SORTED):
        found = sorted_pair(first, lines, rows_refs, 4)
        keys_ref[first : first + SORTED] = found[:, :HEAD].astype(BF16)
        values_ref[:, first : first + SORTED] = found[:, HEAD:].T.astype(BF16)


def sort_keys(rows):
    rounds = len(rows)
    return pl.pallas_call(
        functools.partial(sort_keys_kernel, rounds),
        in_specs=[HERE] * rounds,
        out_specs=(HERE, HERE, HERE, NEAR),
        out_shape=(
            jax.ShapeDtypeStruct((SEQ_BLOCKS, HEAD), BF16),
            jax.ShapeDtypeStruct((HEAD, SEQ_BLOCKS), BF16),
            jax.ShapeDtypeStruct((rounds, HEAD, HEAD), F32),
            jax.ShapeDtypeStruct((1,), jnp.int32),
        ),
        compiler_params=ROOM,
        name="sort_keys",
    )(*rows)


def sort_queries_kernel(*refs):
    rows_refs, out_ref = refs[:-1], refs[-1]
    lines = [line_up(slot_positions(turn, rows_refs[0])) for turn in range(len(rows_refs))]
    for first in range(0, SEQ_BLOCKS, SORTED):
        for c in range(0, 4, 2):
            found = sorted_pair(first, lines, rows_refs, c).astype(BF16)
            out_ref[c, first : first + SORTED] = found[:, :HEAD]
            out_ref[c + 1, first : first + SORTED] = found[:, HEAD:]


def sort_queries(rows):
    flops = 2 * SEQ_BLOCKS * DEVICES * CAP * len(rows) * 4 * HEAD
    return pl.pallas_call(
        sort_queries_kernel,
        in_specs=[HERE] * len(rows),
        out_specs=HERE,
        out_shape=jax.ShapeDtypeStruct((4, SEQ_BLOCKS, HEAD), BF16),
        compiler_params=ROOM,
        cost_estimate=pl.CostEstimate(flops=flops, bytes_accessed=4 << 20, transcendentals=0),
        name="sort_queries",
    )(*rows)


def attend_tile(
    shift, tile, facts_ref, q_ref, own_keys, own_values, other_keys, other_values, out_ref, sum_ref, extra_ref
):
    core = facts_ref[0]
    span = 2 * TILE
    columns = 4 * TILE
    first = tile * span
    queries_ref = q_ref.at[:, pl.ds(pl.multiple_of(tile * TILE, TILE), TILE), :]

    def start_of(position):
        start, end = jnp.zeros_like(position), jnp.int32(0)
        for d in range(1, facts_ref.shape[0]):
            end = end + facts_ref[d]
            start = jnp.where(end <= position, end, start)
        return start

    column = lax.broadcasted_iota(jnp.int32, (1, columns), 1)
    query_pos = first + (column % TILE) * 2 + column // (2 * TILE)
    query_start = start_of(query_pos)

    def key_pos(at, wide, index):
        own = index < wide * TILE
        block = jnp.where(own, index, index - wide * TILE) + at * TILE
        return block * 2 + jnp.where(own, core, 1 - core)

    def scores_of(at, wide):
        at_keys = pl.ds(pl.multiple_of(at * TILE, TILE), wide * TILE)
        keys = jnp.concatenate([own_keys[at_keys, :], other_keys[at_keys, :]], axis=0)
        scores = lax.dot_general(
            keys,
            queries_ref[...].reshape(columns, HEAD),
            (((1,), (1,)), ((), ())),
            preferred_element_type=F32,
        )
        return scores * SCALE

    def allowed_scores(at, whole):
        pos = key_pos(at, 1, lax.broadcasted_iota(jnp.int32, (span, 1), 0))
        allowed = (pos <= query_pos) & (pos >= query_start) if whole else pos <= query_pos
        return jnp.where(allowed, scores_of(at, 1), -1e30)

    def mixed(at, wide, weights, start=None):
        at_keys = pl.ds(pl.multiple_of(at * TILE, TILE), wide * TILE)
        values = jnp.concatenate([own_values[:, at_keys], other_values[:, at_keys]], axis=1)
        ones = jnp.ones((16, wide * span), BF16)
        if start is not None:
            pos = key_pos(at, wide, lax.broadcasted_iota(jnp.int32, (16, wide * span), 1))
            ones = jnp.where(pos >= start, 1.0, 0.0).astype(BF16)
            values = values * ones[0:1]
        values = jnp.concatenate([values, ones], axis=0)
        return jnp.dot(values, weights.astype(BF16), preferred_element_type=F32)

    def own_tile_weights():
        scores = scores_of(tile, 1)
        key_at = lax.broadcasted_iota(jnp.int32, (HEAD, HEAD), 0) * 2
        query_at = lax.broadcasted_iota(jnp.int32, (HEAD, HEAD), 1) * 2
        lines = []
        for k in range(span // HEAD):
            gap = query_at - key_at - (core if k < TILE // HEAD else 1 - core)
            line = []
            for c in range(columns // HEAD):
                piece = scores[k * HEAD : (k + 1) * HEAD, c * HEAD : (c + 1) * HEAD]
                ahead = k % (TILE // HEAD) - c % (TILE // HEAD)
                if ahead > 0:
                    line.append(jnp.zeros((HEAD, HEAD), BF16))
                elif ahead < 0:
                    line.append(jnp.exp2(piece).astype(BF16))
                else:
                    seen = gap + c // (2 * TILE // HEAD) >= 0
                    line.append(jnp.where(seen, jnp.exp2(piece), 0.0).astype(BF16))
            lines.append(jnp.concatenate(line, axis=1))
        return jnp.concatenate(lines, axis=0)

    start = start_of(first)
    low = start // span

    if shift:

        def shifted(at, begins):
            scores = allowed_scores(at, True)
            best = jnp.broadcast_to(jnp.max(scores, axis=0, keepdims=True), (8, columns))
            top = best if begins else jnp.maximum(extra_ref[...], best)
            added = mixed(at, 1, jnp.exp2(scores - top[0:1]))
            if begins:
                sum_ref[...] = added
            else:
                sum_ref[...] = sum_ref[...] * jnp.exp2(extra_ref[0:1] - top[0:1]) + added
            extra_ref[...] = top

        shifted(tile, True)

        @pl.loop(low, tile)
        def _(at):
            shifted(at, False)

    else:
        split = start_of(first + span - 1) > first

        @pl.when(split)
        def _():
            sum_ref[...] = mixed(tile, 1, jnp.exp2(allowed_scores(tile, True)))

        @pl.when(jnp.logical_not(split))
        def _():
            sum_ref[...] = mixed(tile, 1, own_tile_weights())

        left = tile - low
        for wide in (1, 2, 4):

            @pl.when((left // wide) % 2 == 1)
            def _():
                at = low + left % wide
                added = mixed(at, wide, jnp.exp2(scores_of(at, wide)), start)
                sum_ref[...] += jnp.where(query_start <= first, added, 0.0)

        total = sum_ref[HEAD : HEAD + 8]
        extra_ref[...] += jnp.where((total <= 2.0**100) & (total >= 2.0**-80), 0.0, 1.0)

    done = (sum_ref[:HEAD] * (1.0 / sum_ref[HEAD : HEAD + 8])[0:1]).astype(BF16)
    place = pl.ds(pl.multiple_of(tile * TILE, TILE), TILE)
    for c in range(4):
        out_ref[c * HEAD : (c + 1) * HEAD, place] = done[:, c * TILE : (c + 1) * TILE]


def unsort_tile(turn, near, column_ref, attended_ref, out_ref):
    lane = lax.broadcasted_iota(jnp.int32, (HEAD, HEAD), 1)
    wide = UNSORTED // HEAD
    columns = [
        jnp.sum(jnp.where(lane == near * wide + j, column_ref[turn], 0.0), axis=1, keepdims=True)
        for j in range(wide)
    ]
    pos = jnp.concatenate(columns, axis=0).astype(jnp.int32)
    block = lax.broadcasted_iota(jnp.int32, (UNSORTED, SEQ_BLOCKS), 1)
    pick = jnp.where(pos == block, 1.0, 0.0).astype(BF16)
    for c in range(0, 4, 2):
        found = lax.dot_general(
            pick,
            attended_ref[c * HEAD : (c + 2) * HEAD, :],
            (((1,), (1,)), ((), ())),
            preferred_element_type=F32,
        ).astype(BF16)
        for p in range(2):
            part = found[:, p * HEAD : (p + 1) * HEAD].reshape(UNSORTED // CAP, CAP, HEAD)
            devices = slice((turn * UNSORTS + near) * UNSORTED // CAP, (turn * UNSORTS + near + 1) * UNSORTED // CAP)
            out_ref[devices, (c + p) * CAP : (c + p + 1) * CAP, :] = part


def attend_kernel(facts_ref, column_ref, q_ref, *refs):
    key_refs, out_ref, attended_ref, more = refs[:4], refs[4], refs[5], refs[6:]

    def attend_tiles(shift):
        @pl.loop(0, TILES)
        def _(tile):
            attend_tile(shift, tile, facts_ref, q_ref, *key_refs, attended_ref, *more)

    extra_ref = more[1]
    extra_ref[...] = jnp.zeros_like(extra_ref)
    attend_tiles(False)

    @pl.when(jnp.max(extra_ref[...]) > 0.0)
    def _():
        attend_tiles(True)

    for turn in range(column_ref.shape[0]):
        for near in range(UNSORTS):
            unsort_tile(turn, near, column_ref, attended_ref, out_ref)


def attend(facts, column, queries, own, other):
    return pl.pallas_call(
        attend_kernel,
        in_specs=[NEAR] + [HERE] * 6,
        out_specs=HERE,
        out_shape=jax.ShapeDtypeStruct((column.shape[0] * DEVICES, BACK, HEAD), BF16),
        scratch_shapes=[
            pltpu.VMEM((4 * HEAD, SEQ_BLOCKS), BF16),
            pltpu.VMEM((HEAD + 16, 4 * TILE), F32),
            pltpu.VMEM((8, 4 * TILE), F32),
        ],
        compiler_params=ROOM,
        name="attend",
    )(facts, column, queries, *own, *other)


def unpack_kernel(rounds, *refs):
    place_refs, back_refs, out_ref = refs[:rounds], refs[rounds:-1], refs[-1]
    total = jnp.zeros(out_ref.shape, F32)
    for turn in range(rounds):
        lines = []
        for parity in range(2):
            for i in range(INSTANCES):
                line = []
                for g in range(GROUP):
                    for r in range(4):
                        of = (i // 2, r % 2, i % 2, g, r // 2)
                        for h in range(2):
                            at = (2 * parity + h) * CAP
                            line.append(back_refs[turn][(*of, slice(at, at + CAP), slice(None))])
                lines.append(jnp.concatenate(line, axis=1))
        total = total + jnp.dot(
            place_refs[turn][...], jnp.concatenate(lines, axis=0), preferred_element_type=F32
        )
    out_ref[...] = total.astype(BF16)


def unpack(places, backs):
    rounds = len(backs)
    block = pl.BlockSpec((2, 2, 2, GROUP, 2, BACK, HEAD), lambda g: (0, 0, 0, g, 0, 0, 0))
    return pl.pallas_call(
        functools.partial(unpack_kernel, rounds),
        grid=(KEY_HEADS // GROUP,),
        in_specs=[pl.BlockSpec((ROWS, ROWS), lambda g: (0, 0))] * rounds + [block] * rounds,
        out_specs=pl.BlockSpec((ROWS, WIDE), lambda g: (0, g)),
        out_shape=jax.ShapeDtypeStruct((ROWS, KEY_HEADS * 8 * HEAD), BF16),
        compiler_params=ROOM,
        name="unpack",
    )(*places, *(b.reshape(2, 2, 2, KEY_HEADS, 2, BACK, HEAD) for b in backs))


def exchange(x):
    return lax.all_to_all(x, BOTH, split_axis=0, concat_axis=0, tiled=True)


def shards(query_rows, key_rows, value_rows, target_instance, block_position, request_lengths):
    spot, place = lax.axis_index("inst"), lax.axis_index("seq")
    core = spot % 2
    instance = (spot // 2) * 2 + place // 16
    lengths = lax.dynamic_index_in_dim(request_lengths, instance, 0, keepdims=False)
    facts = jnp.concatenate([core[None], lengths]).astype(jnp.int32)
    plan = ((place % 8 * CAP)[None], target_instance[None, :], block_position[None, :])

    def run(rounds):
        packed = [pack(t, *plan, query_rows, key_rows, value_rows) for t in range(rounds)]
        rows = [exchange(sent) for sent, _ in packed]
        keys, values, column, most = sort_keys(rows)
        pairs = [(0, 1), (1, 0), (2, 3), (3, 2)]
        other = [lax.ppermute(x, "inst", pairs) for x in (keys, values)]
        back = attend(facts, column, sort_queries(rows), (keys, values), other)
        backs = [exchange(back[t * DEVICES : (t + 1) * DEVICES]) for t in range(rounds)]
        return unpack([places for _, places in packed], backs), most[0]

    attended, most = run(1)
    return lax.while_loop(
        lambda state: state[1] > CAP,
        lambda state: (run(2)[0], jnp.zeros_like(state[1])),
        (attended, most),
    )[0]


def solution(mesh):
    rows = P(BOTH, None)
    return jax.shard_map(
        shards,
        mesh=mesh,
        in_specs=(rows, rows, rows, P(BOTH), P(BOTH), P()),
        out_specs=rows,
        check_vma=False,
    )
```
